32 devices in a mesh: leaf: 32 (over z, y, x, core).
Axes of the slice: x: 2, y: 2, z: 4, core: 2. Of those that a mesh axis runs over, the one named last changes fastest.
Arguments:
- points: bfloat16 [128, 262144], P(None, 'leaf')
- probes: bfloat16 [16, 262144], P(None, 'leaf'), may hold values from -6 to 6
- near_list: int32 [512, 4], P('leaf'), may hold values from 0 to 511, as said below
- near_count: int32 [512], P('leaf'), may hold values from 1 to 4, as said below
- leaf_skel: int32 [512, 128], P('leaf'), may hold values from 0 to 511, as said below
- local_skel: int32 [480, 128], P('leaf'), may hold values from 0 to 255, as said below
- upper_skel: int32 [31, 128], replicated, may hold values from 0 to 255, as said below
Outputs:
- response: float32 [16, 262144], P(None, 'leaf')
The draws below stay inside these ranges and needn't reach their ends.
Inputs may be any that keep to these rules, and one draw needn't show every extreme that they name: `near_list`: entry 0 of leaf t's list is t itself; every entry is a leaf of the same block of 16 consecutive leaves as t, or of the block just before or just after it. `near_count`: some leaf uses all 4 slots. `leaf_skel`: each row holds 128 distinct values. `local_skel`: each row holds 128 distinct values. `upper_skel`: each row holds 128 distinct values.
All inputs are finite; a program needn't handle non-finite values.
Results may differ from the reference program's by a relative error of at most 0.0015.
Values may be sent and summed in bfloat16 or wider, within the bound.
A program may use at most 128 MiB of HBM per device.

```python
import jax
import jax.numpy as jnp
from jax import lax

D = 128
PROBES = 16
LEAF = 512
SKEL = 128
NEAR = 4
LOC_LEVELS = 4
LEAF_DEV = 16
LEAVES = 512
POINTS = 262144
LOCAL_NODES = 480
UPPER_NODES = 31
N_LEAF = 32


def draw_points(key, part):
    shape = (D, POINTS)
    values = jax.random.normal(key, shape, jnp.float32)
    return values.astype(jnp.bfloat16)


def near_tables(key):
    base = jax.random.fold_in(key, 11)
    key_dev, key_leaf, key_top, key_count = jax.random.split(base, 4)
    leaf_ids = jnp.arange(LEAVES, dtype=jnp.int32)
    group_of = leaf_ids // LEAF_DEV
    group_num = LEAVES // LEAF_DEV
    hop_dir = jax.random.randint(key_dev, (LEAVES, NEAR), -1, 2, dtype=jnp.int32)
    src_group = jnp.clip(group_of[:, None] + hop_dir, 0, group_num - 1)
    src_leaf = jax.random.randint(key_leaf, (LEAVES, NEAR), 0, LEAF_DEV, dtype=jnp.int32)
    listed = src_group * LEAF_DEV + src_leaf
    before_group = jnp.where(group_of > 0, group_of - 1, group_of + 1)
    after_group = jnp.where(group_of < group_num - 1, group_of + 1, group_of - 1)
    listed = listed.at[:, 1].set(before_group * LEAF_DEV + src_leaf[:, 1])
    listed = listed.at[:, 2].set(after_group * LEAF_DEV + src_leaf[:, 2])
    listed = listed.at[:, 0].set(leaf_ids)
    ceiling = jax.random.randint(key_top, (group_num,), 2, NEAR + 1, dtype=jnp.int32)[group_of]
    counts = jax.random.randint(key_count, (LEAVES,), 1, ceiling + 1, dtype=jnp.int32)
    counts = jnp.where(leaf_ids % LEAF_DEV == 0, NEAR, counts).astype(jnp.int32)
    return (listed.astype(jnp.int32), counts)


def draw_near_list(key, part):
    return near_tables(key)[0]


def draw_near_count(key, part):
    return near_tables(key)[1]


def pick_rows(key, row_num, pool):
    row_keys = jax.random.split(key, row_num)
    picked = jax.vmap(lambda row_key: jax.random.permutation(row_key, pool)[:SKEL])(row_keys)
    return picked.astype(jnp.int32)


def draw_leaf_skel(key, part):
    return pick_rows(jax.random.fold_in(key, 21), LEAVES, LEAF)


def draw_local_skel(key, part):
    return pick_rows(jax.random.fold_in(key, 22), LOCAL_NODES, 2 * SKEL)


def draw_upper_skel(key, part):
    return pick_rows(jax.random.fold_in(key, 23), UPPER_NODES, 2 * SKEL)


def shard_levels(rng, extent, shards, least, largest):
    def one(dim, shards_of):
        draws = jax.random.uniform(jax.random.fold_in(jax.random.fold_in(rng, 6), dim), (shards_of,), jnp.float32, least / len(shards), largest / len(shards))
        return jnp.repeat(jnp.exp(draws), extent[dim] // shards_of).reshape((-1,) + (1,) * (len(extent) - dim - 1))

    loudness = one(*shards[0])
    for cut in shards[1:]:
        loudness = loudness * one(*cut)
    return loudness


def scatter_about(rng, shape, width, limit, shards=(), held_as=jnp.bfloat16):
    array = jax.random.normal(rng, shape, jnp.float32) * width
    if len(shards) > 0:
        array = shard_levels(rng, shape, shards, -0.22, 0.18) * array
    return jnp.clip(array, min=-limit, max=limit).astype(held_as)


def setup_inputs(seed: int = 0) -> dict:
    key_list = jax.random.split(jax.random.key(seed), 8)
    points = draw_points(jax.random.fold_in(key_list[7], 71), 0)
    probes = scatter_about(key_list[1], (PROBES, POINTS), 1.0, 6.0, ((1, 32),))
    near_list = draw_near_list(jax.random.fold_in(key_list[7], 71), 0)
    near_count = draw_near_count(jax.random.fold_in(key_list[7], 71), 0)
    leaf_skel = draw_leaf_skel(jax.random.fold_in(key_list[7], 71), 0)
    local_skel = draw_local_skel(jax.random.fold_in(key_list[7], 71), 0)
    upper_skel = draw_upper_skel(jax.random.fold_in(key_list[7], 71), 0)
    return {"points": points, "probes": probes, "near_list": near_list, "near_count": near_count, "leaf_skel": leaf_skel, "local_skel": local_skel, "upper_skel": upper_skel}


HIGH = lax.Precision.HIGHEST


def kernel_block(left_pts, right_pts):
    left_wide = left_pts.astype(jnp.float32)
    right_wide = right_pts.astype(jnp.float32)
    left_sq = jnp.sum(left_wide * left_wide, axis=0)
    right_sq = jnp.sum(right_wide * right_wide, axis=0)
    inner_prod = jnp.dot(left_wide.T, right_wide, precision=HIGH)
    distance = left_sq[:, None] + right_sq[None, :] - 2.0 * inner_prod
    return jnp.exp(distance * (-2.0 / left_pts.shape[0]))


def kernel_batch(left_pts, right_pts):
    return jax.vmap(kernel_block)(left_pts, right_pts)


def up_level(child_pts, child_q, chosen):
    node_num, skel_len = chosen.shape
    emb_width = child_pts.shape[1]
    probe_num = child_q.shape[1]
    paired_pts = child_pts.reshape(node_num, 2, emb_width, skel_len)
    paired_q = child_q.reshape(node_num, 2, probe_num, skel_len).astype(jnp.float32)
    first_pts = paired_pts[:, 0]
    second_pts = paired_pts[:, 1]
    first_q = paired_q[:, 0]
    second_q = paired_q[:, 1]
    cross_k = kernel_batch(first_pts, second_pts)
    couple_first = jnp.einsum("npj,nij->npi", second_q, cross_k, precision=HIGH)
    couple_second = jnp.einsum("npi,nij->npj", first_q, cross_k, precision=HIGH)
    coupling = jnp.stack([couple_first, couple_second], axis=1).reshape(2 * node_num, probe_num, skel_len)
    joined_pts = jnp.concatenate([first_pts, second_pts], axis=2)
    joined_q = jnp.concatenate([first_q, second_q], axis=2)
    parent_pts = jnp.take_along_axis(joined_pts, chosen[:, None, :], axis=2)
    up_kernel = kernel_batch(joined_pts, parent_pts)
    parent_q = jnp.einsum("npc,ncs->nps", joined_q, up_kernel, precision=HIGH).astype(jnp.bfloat16)
    return parent_pts, parent_q, up_kernel, coupling


def descend(down_field, up_kernel, coupling):
    node_num, probe_num, skel_len = down_field.shape
    spread = jnp.einsum("nps,ncs->npc", down_field, up_kernel, precision=HIGH)
    spread = spread.reshape(node_num, probe_num, 2, skel_len).transpose(0, 2, 1, 3)
    return spread.reshape(2 * node_num, probe_num, skel_len) + coupling


def reference(points, probes, near_list, near_count, leaf_skel, local_skel, upper_skel):
    leaf_tiles = points.reshape(D, LEAVES, LEAF)
    probe_tiles = probes.reshape(PROBES, LEAVES, LEAF)
    leaf_ids = jnp.arange(LEAVES, dtype=jnp.int32)

    def near_leaf(leaf_id):
        target = leaf_tiles[:, leaf_id]
        sources = near_list[leaf_id]
        src_pts = jnp.take(leaf_tiles, sources, axis=1)
        src_prb = jnp.take(probe_tiles, sources, axis=1).astype(jnp.float32)
        blocks = jax.vmap(kernel_block, in_axes=(None, 1))(target, src_pts)
        blocks = lax.optimization_barrier(blocks.astype(jnp.bfloat16)).astype(jnp.float32)
        contrib = jnp.einsum("pms,mts->mpt", src_prb, blocks, precision=HIGH)
        is_live = jnp.arange(NEAR, dtype=jnp.int32) < near_count[leaf_id]
        return jnp.sum(jnp.where(is_live[:, None, None], contrib, jnp.zeros_like(contrib)), axis=0)

    near_part = lax.map(near_leaf, leaf_ids)

    def leaf_up(leaf_id):
        target = leaf_tiles[:, leaf_id]
        skel_pts = jnp.take(target, leaf_skel[leaf_id], axis=1)
        leaf_kernel = kernel_block(target, skel_pts)
        charge = jnp.dot(probe_tiles[:, leaf_id].astype(jnp.float32), leaf_kernel, precision=HIGH)
        return skel_pts, charge.astype(jnp.bfloat16)

    node_pts, node_q = lax.map(leaf_up, leaf_ids)
    sections = []
    local_rows = local_skel.reshape(N_LEAF, LEAF_DEV - 1, SKEL)
    for level_no in range(1, LOC_LEVELS + 1):
        offset = LEAF_DEV - (LEAF_DEV >> (level_no - 1))
        chosen = local_rows[:, offset:offset + (LEAF_DEV >> level_no)].reshape(-1, SKEL)
        node_pts, node_q, up_kernel, coupling = up_level(node_pts, node_q, chosen)
        sections.append((up_kernel, coupling))
    for bit_no in range(N_LEAF.bit_length() - 1):
        offset = N_LEAF - (N_LEAF >> bit_no)
        chosen = upper_skel[offset:offset + (N_LEAF >> (bit_no + 1))]
        node_pts, node_q, up_kernel, coupling = up_level(node_pts, node_q, chosen)
        sections.append((up_kernel, coupling))
    down_field = jnp.zeros((1, PROBES, SKEL), jnp.float32)
    for up_kernel, coupling in reversed(sections):
        down_field = descend(down_field, up_kernel, coupling)

    def leaf_down(inputs):
        leaf_id, field_row = inputs
        target = leaf_tiles[:, leaf_id]
        skel_pts = jnp.take(target, leaf_skel[leaf_id], axis=1)
        leaf_kernel = kernel_block(target, skel_pts)
        return jnp.dot(field_row, leaf_kernel.T, precision=HIGH)

    far_part = lax.map(leaf_down, (leaf_ids, down_field))
    response = near_part + far_part
    return jnp.transpose(response, (1, 0, 2)).reshape(PROBES, POINTS)
```

```python
import functools
import math

import jax
import jax.numpy as jnp
from jax import lax
from jax.experimental import pallas as pl
from jax.experimental.pallas import tpu as pltpu
from jax.sharding import PartitionSpec as P

F32 = jnp.float32
BF16 = jnp.bfloat16
DEEP = 256
PIECE = 16
PAIRS = 2
VMEM_LIMIT = 56 * 1024 * 1024


def mm(left, right):
    return jnp.dot(left, right, preferred_element_type=F32)


def mm_nt(left, right):
    return lax.dot_general(left, right, (((1,), (1,)), ((), ())), preferred_element_type=F32)


def split(value):
    high = value.astype(BF16)
    low = (value - high.astype(F32)).astype(BF16)
    return high, low


def affinity(scaled, emb_width):
    return jnp.exp2(scaled * (4.0 / emb_width * math.log2(math.e)))


def half_norms(pts):
    wide = pts.astype(F32)
    value = jnp.sum(wide * wide, axis=0, keepdims=True) * -0.5
    first = value.astype(BF16).astype(F32)
    rest = value - first
    second = rest.astype(BF16).astype(F32)
    third = (rest - second).astype(BF16).astype(F32)
    return first, second, third


def norm_rows(pieces, start):
    width = pieces[0].shape[1]
    row = lax.broadcasted_iota(jnp.int32, (PIECE, width), 0)
    rows = jnp.where(row < 6, 1.0, 0.0)
    for k, piece in enumerate(pieces):
        rows = jnp.where(row == start + k, piece, rows)
    return rows.astype(BF16)


def deep(*blocks):
    rows = sum(block.shape[0] for block in blocks)
    filler = jnp.zeros((DEEP - rows, blocks[0].shape[1]), BF16)
    return jnp.concatenate([*blocks, filler], axis=0)


def one_hot(pool, chosen):
    column = lax.broadcasted_iota(jnp.int32, (pool, chosen.shape[1]), 0)
    return jnp.where(column == chosen, 1.0, 0.0).astype(BF16)


def in_groups(total, size, step):
    size = min(size, total)
    if size == total:
        step(list(range(total)))
        return

    def body(i, carry):
        step([i * size + k for k in range(size)])
        return carry

    lax.fori_loop(0, total // size, body, 0)


def tree_node(first, second, first_q, second_q, chosen, emb_width, coupled):
    skel = first.shape[1]
    right_end = emb_width + PIECE
    joined = jnp.concatenate([first, second], axis=1)
    parent = mm(joined, one_hot(2 * skel, chosen)).astype(BF16)
    left = deep(joined[:emb_width], joined[right_end:]).T
    if coupled:
        right = deep(jnp.concatenate([parent[:right_end], second[:right_end]], axis=1))
    else:
        right = deep(parent[:right_end])
    raw = mm(left, right)
    up_high, up_low = split(affinity(raw[:, :skel], emb_width))
    joined_q = jnp.concatenate([first_q, second_q], axis=1)
    parent_q = (mm(joined_q, up_high) + mm(joined_q, up_low)).astype(BF16)
    if not coupled:
        return parent, parent_q
    cross_high, cross_low = split(affinity(raw[:skel, skel:], emb_width))
    couple_first = mm_nt(second_q, cross_high) + mm_nt(second_q, cross_low)
    couple_second = mm(first_q, cross_high) + mm(first_q, cross_low)
    return parent, parent_q, up_high, up_low, couple_first, couple_second


def spread_down(field, up_high, up_low):
    rows = field.shape[0]
    high, low = split(field)
    both = mm_nt(jnp.concatenate([high, low], axis=0), up_high)
    return both[:rows] + both[rows:] + mm_nt(high, up_low)


def up_body(pts, prb, leaf_skel, local_skel, left_out, right_out, lk_high, lk_low, up_high, up_low, couple, root, nodes, node_q):
    emb_width = pts.shape[0]
    leaf_dev, skel = leaf_skel.shape
    leaf_len = pts.shape[1] // leaf_dev

    def leaf_step(ids):
        done = []
        for i in ids:
            span = pl.ds(pl.multiple_of(i * leaf_len, leaf_len), leaf_len)
            tile = pts[:, span]
            pieces = half_norms(tile)
            right_rows = norm_rows(pieces, 3)
            left_rows = norm_rows(pieces, 0)
            left = deep(tile, left_rows).T
            stacked = jnp.concatenate([tile, right_rows, left_rows], axis=0)
            node = mm(stacked, one_hot(leaf_len, leaf_skel[pl.ds(i, 1), :])).astype(BF16)
            raw = mm(left, deep(node[: emb_width + PIECE]))
            high, low = split(affinity(raw, emb_width))
            tile_prb = prb[:, span]
            charge = (mm(tile_prb, high) + mm(tile_prb, low)).astype(BF16)
            done.append((span, right_rows, left, node, high, low, charge))
        for i, (span, right_rows, left, node, high, low, charge) in zip(ids, done):
            left_out[span, :] = left
            right_out[:, span] = right_rows
            lk_high[span, :] = high
            lk_low[span, :] = low
            nodes[i] = node
            node_q[i] = charge

    in_groups(leaf_dev, 4, leaf_step)
    count = leaf_dev // 2
    row_base = 0
    while count:

        def level_step(ids, row_base=row_base):
            done = []
            for k in ids:
                row = row_base + k
                done.append(
                    tree_node(
                        nodes[2 * row], nodes[2 * row + 1], node_q[2 * row], node_q[2 * row + 1],
                        local_skel[pl.ds(row, 1), :], emb_width, True,
                    )
                )
            for k, (parent, parent_q, high, low, one, two) in zip(ids, done):
                row = row_base + k
                nodes[leaf_dev + row] = parent
                node_q[leaf_dev + row] = parent_q
                up_high[row] = high
                up_low[row] = low
                couple[2 * row] = one
                couple[2 * row + 1] = two

        in_groups(count, 4, level_step)
        row_base += count
        count //= 2
    top = 2 * leaf_dev - 2
    rows = nodes.shape[1]
    root[:rows, :] = nodes[top]
    root[rows:, :] = node_q[top]


def list_pairs(near_list, near_count, base, leaf_dev, targets, sources):
    def of_leaf(leaf, found):
        def of_slot(slot, found):
            source = near_list[leaf, slot] - base
            targets[found] = leaf
            sources[found] = jnp.clip(source, 0, leaf_dev - 1)
            inside = jnp.logical_and(source >= 0, source < leaf_dev)
            return found + jnp.where(inside, 1, 0)

        return lax.fori_loop(0, near_count[leaf], of_slot, found)

    found = lax.fori_loop(0, leaf_dev, of_leaf, 0)
    for k in range(PAIRS - 1):
        targets[found + k] = leaf_dev
        sources[found + k] = 0
    return (found + PAIRS - 1) // PAIRS


def add_pairs(steps, targets, sources, left, pts, rows, prb, total):
    emb_width = pts.shape[0]
    leaf_dev = total.shape[0] - 1
    leaf_len = total.shape[2]
    chunk = min(256, leaf_len)

    def step(i, carry):
        done = []
        for k in range(PAIRS):
            target = targets[i * PAIRS + k]
            start = pl.multiple_of(sources[i * PAIRS + k] * leaf_len, leaf_len)
            span = pl.ds(start, leaf_len)
            right = deep(pts[:, span], rows[:, span])
            source_prb = prb[:, span]
            left_at = jnp.minimum(target, leaf_dev - 1) * leaf_len
            for at in range(0, leaf_len, chunk):
                part = left[pl.ds(pl.multiple_of(left_at + at, chunk), chunk), :]
                block = affinity(mm(part, right), emb_width).astype(BF16)
                done.append((target, at, mm_nt(source_prb, block)))
        for target, at, term in done:
            total[target, :, at : at + chunk] += term
        return carry

    lax.fori_loop(0, steps, step, 0)


def near_own_body(me, near_list, near_count, left, pts, rows, prb, total, targets, sources):
    leaf_dev = near_list.shape[0]
    total[...] = jnp.zeros_like(total)
    steps = list_pairs(near_list, near_count, me[0] * leaf_dev, leaf_dev, targets, sources)
    add_pairs(steps, targets, sources, left, pts, rows, prb, total)


def near_halo_body(me, near_list, near_count, left, pts_a, prb_a, pts_b, prb_b, so_far, far, out, total, rows_a, rows_b, targets, sources):
    leaf_dev = near_list.shape[0]
    leaf_len = total.shape[2]
    total[...] = so_far[...]
    for pts, rows in ((pts_a, rows_a), (pts_b, rows_b)):

        def norms(ids, pts=pts, rows=rows):
            for i in ids:
                span = pl.ds(pl.multiple_of(i * leaf_len, leaf_len), leaf_len)
                rows[:, span] = norm_rows(half_norms(pts[:, span]), 3)

        in_groups(leaf_dev, 2, norms)
    for shift, pts, rows, prb in ((-1, pts_a, rows_a, prb_a), (1, pts_b, rows_b, prb_b)):
        steps = list_pairs(near_list, near_count, (me[0] + shift) * leaf_dev, leaf_dev, targets, sources)
        add_pairs(steps, targets, sources, left, pts, rows, prb, total)
    for leaf in range(leaf_dev):
        span = slice(leaf * leaf_len, (leaf + 1) * leaf_len)
        out[:, span] = total[leaf] + far[:, span]


def down_body(emb_width, me, roots, upper_skel, lk_high, lk_low, up_high, up_low, couple, far, nodes, path_high, path_low, path_couple, fields):
    dev_num = roots.shape[0]
    skel = upper_skel.shape[1]
    pts_rows = emb_width + 2 * PIECE
    leaf_dev = couple.shape[0] // 2 + 1
    leaf_len = lk_high.shape[0] // leaf_dev
    mine = me[0]
    levels = dev_num.bit_length() - 1
    for level in range(levels):
        row_base = dev_num - (dev_num >> level)
        children = roots if level == 0 else nodes
        child_base = 0 if level == 0 else dev_num - (dev_num >> (level - 1))

        def operands(k, level=level, row_base=row_base, children=children, child_base=child_base):
            one = children[child_base + 2 * k]
            two = children[child_base + 2 * k + 1]
            chosen = upper_skel[pl.ds(row_base + k, 1), :]
            return one[:pts_rows], two[:pts_rows], one[pts_rows:], two[pts_rows:], chosen

        spot = jnp.right_shift(mine, level + 1)
        bit = jnp.bitwise_and(jnp.right_shift(mine, level), 1)
        _, _, high, low, couple_one, couple_two = tree_node(*operands(spot), emb_width, True)
        path_high[level] = high
        path_low[level] = low
        path_couple[level] = jnp.where(bit == 0, couple_one, couple_two)

        if level < levels - 1:

            def level_step(ids, row_base=row_base, operands=operands):
                done = [tree_node(*operands(k), emb_width, False) for k in ids]
                for k, (parent, parent_q) in zip(ids, done):
                    nodes[row_base + k, :pts_rows, :] = parent
                    nodes[row_base + k, pts_rows:, :] = parent_q

            in_groups(dev_num >> (level + 1), 4, level_step)
    field = jnp.zeros(path_couple.shape[1:], F32)
    for level in reversed(range(levels)):
        bit = jnp.bitwise_and(jnp.right_shift(mine, level), 1)
        spread = spread_down(field, path_high[level], path_low[level])
        field = jnp.where(bit == 0, spread[:, :skel], spread[:, skel:]) + path_couple[level]
    top = 2 * leaf_dev - 2
    fields[top] = field
    count = 1
    row_base = leaf_dev - 2
    while count < leaf_dev:

        def level_step(ids, row_base=row_base):
            done = []
            for k in ids:
                row = row_base + k
                spread = spread_down(fields[leaf_dev + row], up_high[row], up_low[row])
                done.append((spread[:, :skel] + couple[2 * row], spread[:, skel:] + couple[2 * row + 1]))
            for k, (one, two) in zip(ids, done):
                fields[2 * (row_base + k)] = one
                fields[2 * (row_base + k) + 1] = two

        in_groups(count, 4, level_step)
        count *= 2
        row_base -= count

    def leaf_step(ids):
        for i in ids:
            span = pl.ds(pl.multiple_of(i * leaf_len, leaf_len), leaf_len)
            far[:, span] = spread_down(fields[i], lk_high[span, :], lk_low[span, :])

    in_groups(leaf_dev, 4, leaf_step)


def shape(dims, dtype):
    return jax.ShapeDtypeStruct(tuple(dims), dtype)


def call(body, name, operands, outs, scratch, scalars, flops, exps):
    vmem = pl.BlockSpec(memory_space=pltpu.VMEM)
    smem = pl.BlockSpec(memory_space=pltpu.SMEM)
    moved = sum(x.size * x.dtype.itemsize for x in [*operands, *outs])
    return pl.pallas_call(
        body,
        out_shape=outs,
        in_specs=[smem] * scalars + [vmem] * (len(operands) - scalars),
        out_specs=[vmem] * len(outs),
        scratch_shapes=scratch,
        compiler_params=pltpu.CompilerParams(vmem_limit_bytes=VMEM_LIMIT),
        cost_estimate=pl.CostEstimate(flops=flops, bytes_accessed=moved, transcendentals=exps),
        name=name,
    )(*operands)


def per_device(points, probes, near_list, near_count, leaf_skel, local_skel, upper_skel):
    emb_width, shard_len = points.shape
    leaf_dev, slots = near_list.shape
    leaf_len = shard_len // leaf_dev
    skel = leaf_skel.shape[1]
    probe_num = probes.shape[0]
    dev_num = lax.axis_size("leaf")
    levels = dev_num.bit_length() - 1
    me = lax.axis_index("leaf").astype(jnp.int32).reshape(1)
    rise = [(i, i + 1) for i in range(dev_num - 1)]
    fall = [(i + 1, i) for i in range(dev_num - 1)]
    pts_a = lax.ppermute(points, "leaf", rise)
    prb_a = lax.ppermute(probes, "leaf", rise)
    pts_b = lax.ppermute(points, "leaf", fall)
    prb_b = lax.ppermute(probes, "leaf", fall)

    low_nodes = leaf_dev - 1
    all_nodes = 2 * leaf_dev - 1
    pts_rows = emb_width + 2 * PIECE
    left, rows, lk_high, lk_low, up_high, up_low, couple, root = call(
        up_body,
        "leaf_up",
        [points, probes, leaf_skel, local_skel],
        [
            shape((shard_len, DEEP), BF16),
            shape((PIECE, shard_len), BF16),
            shape((shard_len, skel), BF16),
            shape((shard_len, skel), BF16),
            shape((low_nodes, 2 * skel, skel), BF16),
            shape((low_nodes, 2 * skel, skel), BF16),
            shape((2 * low_nodes, probe_num, skel), F32),
            shape((pts_rows + probe_num, skel), BF16),
        ],
        [pltpu.VMEM((all_nodes, pts_rows, skel), BF16), pltpu.VMEM((all_nodes, probe_num, skel), BF16)],
        0,
        8 * shard_len * skel * DEEP,
        shard_len * skel * 2,
    )
    roots = lax.all_gather(root, "leaf")

    pair_len = slots * leaf_dev + PAIRS
    lists = [pltpu.SMEM((pair_len,), jnp.int32), pltpu.SMEM((pair_len,), jnp.int32)]
    pair_cost = 4 * leaf_len * leaf_len * DEEP
    (near_own,) = call(
        near_own_body,
        "near_own",
        [me, near_list, near_count, left, points, rows, probes],
        [shape((leaf_dev + 1, probe_num, leaf_len), F32)],
        lists,
        3,
        pair_cost * leaf_dev * 2,
        leaf_len * leaf_len * leaf_dev * 2,
    )
    (far,) = call(
        functools.partial(down_body, emb_width),
        "tree_down",
        [me, roots, upper_skel, lk_high, lk_low, up_high, up_low, couple],
        [shape((probe_num, shard_len), F32)],
        [
            pltpu.VMEM((dev_num, pts_rows + probe_num, skel), BF16),
            pltpu.VMEM((levels, 2 * skel, skel), BF16),
            pltpu.VMEM((levels, 2 * skel, skel), BF16),
            pltpu.VMEM((levels, probe_num, skel), F32),
            pltpu.VMEM((all_nodes, probe_num, skel), F32),
        ],
        1,
        8 * shard_len * skel * DEEP,
        shard_len * skel,
    )
    (response,) = call(
        near_halo_body,
        "near_halo",
        [me, near_list, near_count, left, pts_a, prb_a, pts_b, prb_b, near_own, far],
        [shape((probe_num, shard_len), F32)],
        [
            pltpu.VMEM((leaf_dev + 1, probe_num, leaf_len), F32),
            pltpu.VMEM((PIECE, shard_len), BF16),
            pltpu.VMEM((PIECE, shard_len), BF16),
            *lists,
        ],
        3,
        pair_cost * leaf_dev * 2,
        leaf_len * leaf_len * leaf_dev * 2,
    )
    return response


def solution(mesh):
    in_specs = (
        P(None, "leaf"),
        P(None, "leaf"),
        P("leaf", None),
        P("leaf"),
        P("leaf", None),
        P("leaf", None),
        P(),
    )
    return jax.shard_map(
        per_device, mesh=mesh, in_specs=in_specs, out_specs=P(None, "leaf"), check_vma=False
    )
```

```python
import math

import jax
import jax.numpy as jnp
from jax import lax
from jax.experimental import pallas as pl
from jax.experimental.pallas import tpu as pltpu
from jax.sharding import PartitionSpec as P

F32 = jnp.float32
BF16 = jnp.bfloat16
DEEP = 256
PIECE = 16
PAIRS = 2
VMEM_LIMIT = 56 * 1024 * 1024
MESH = pl.DeviceIdType.MESH


def mm(left, right):
    return jnp.dot(left, right, preferred_element_type=F32)


def mm_nt(left, right):
    return lax.dot_general(left, right, (((1,), (1,)), ((), ())), preferred_element_type=F32)


def split(value):
    high = value.astype(BF16)
    low = (value - high.astype(F32)).astype(BF16)
    return high, low


def affinity(scaled, emb_width):
    return jnp.exp2(scaled * (4.0 / emb_width * math.log2(math.e)))


def half_norms(pts):
    wide = pts.astype(F32)
    value = jnp.sum(wide * wide, axis=0, keepdims=True) * -0.5
    first = value.astype(BF16).astype(F32)
    rest = value - first
    second = rest.astype(BF16).astype(F32)
    third = (rest - second).astype(BF16).astype(F32)
    return first, second, third


def norm_rows(pieces, start):
    width = pieces[0].shape[1]
    row = lax.broadcasted_iota(jnp.int32, (PIECE, width), 0)
    rows = jnp.where(row < 6, 1.0, 0.0)
    for k, piece in enumerate(pieces):
        rows = jnp.where(row == start + k, piece, rows)
    return rows.astype(BF16)


def deep(*blocks):
    rows = sum(block.shape[0] for block in blocks)
    filler = jnp.zeros((DEEP - rows, blocks[0].shape[1]), BF16)
    return jnp.concatenate([*blocks, filler], axis=0)


def one_hot(pool, chosen):
    column = lax.broadcasted_iota(jnp.int32, (pool, chosen.shape[1]), 0)
    return jnp.where(column == chosen, 1.0, 0.0).astype(BF16)


def in_groups(total, size, step):
    size = min(size, total)
    if size == total:
        step(list(range(total)))
        return

    def body(i, carry):
        step([i * size + k for k in range(size)])
        return carry

    lax.fori_loop(0, total // size, body, 0)


def tree_node(first, second, first_q, second_q, chosen, emb_width):
    skel = first.shape[1]
    right_end = emb_width + PIECE
    joined = jnp.concatenate([first, second], axis=1)
    parent = mm(joined, one_hot(2 * skel, chosen)).astype(BF16)
    left = deep(joined[:emb_width], joined[right_end:]).T
    right = deep(jnp.concatenate([parent[:right_end], second[:right_end]], axis=1))
    raw = mm(left, right)
    up_high, up_low = split(affinity(raw[:, :skel], emb_width))
    joined_q = jnp.concatenate([first_q, second_q], axis=1)
    parent_q = (mm(joined_q, up_high) + mm(joined_q, up_low)).astype(BF16)
    cross_high, cross_low = split(affinity(raw[:skel, skel:], emb_width))
    couple_first = mm_nt(second_q, cross_high) + mm_nt(second_q, cross_low)
    couple_second = mm(first_q, cross_high) + mm(first_q, cross_low)
    return parent, parent_q, up_high, up_low, couple_first, couple_second


def spread_down(field, up_high, up_low):
    rows = field.shape[0]
    high, low = split(field)
    both = mm_nt(jnp.concatenate([high, low], axis=0), up_high)
    return both[:rows] + both[rows:] + mm_nt(high, up_low)


def tree_body(
    pts, prb, leaf_skel, local_skel, upper_skel,
    left, near, far, halo_pts, halo_prb,
    right_rows, lk_high, lk_low, up_high, up_low, couple, nodes, node_q,
    outbox, inbox, path_high, path_low, path_couple, fields,
    own_sem, halo_send, halo_recv, box_send, box_recv,
):
    emb_width = pts.shape[0]
    leaf_dev, skel = leaf_skel.shape
    leaf_len = pts.shape[1] // leaf_dev
    pts_rows = nodes.shape[1]
    levels = inbox.shape[0]
    dev_num = 1 << levels
    mine = lax.axis_index("leaf")
    bits = [lax.rem(lax.div(mine, 1 << level), 2) for level in range(levels)]
    partners = [mine + (1 - 2 * bits[level]) * (1 << level) for level in range(levels)]

    barrier = pltpu.get_barrier_semaphore()
    for peer in partners:
        pl.semaphore_signal(barrier, inc=1, device_id=(peer,), device_id_type=MESH)
    has_before = mine > 0
    has_after = mine < dev_num - 1
    crosses_before = jnp.logical_and(has_before, bits[0] == 0)
    crosses_after = jnp.logical_and(has_after, bits[0] == 1)

    @pl.when(crosses_before)
    def _():
        pl.semaphore_signal(barrier, inc=1, device_id=(mine - 1,), device_id_type=MESH)

    @pl.when(crosses_after)
    def _():
        pl.semaphore_signal(barrier, inc=1, device_id=(mine + 1,), device_id_type=MESH)

    pl.semaphore_wait(barrier, levels + jnp.where(jnp.logical_or(crosses_before, crosses_after), 1, 0))

    def halo_copy(which, source, target, slot, peer):
        return pltpu.make_async_remote_copy(
            src_ref=source, dst_ref=target.at[slot], send_sem=halo_send.at[which], recv_sem=halo_recv.at[which],
            device_id=(peer,), device_id_type=MESH,
        )

    to_after = [halo_copy(0, pts, halo_pts, 0, mine + 1), halo_copy(1, prb, halo_prb, 0, mine + 1)]
    to_before = [halo_copy(2, pts, halo_pts, 2, mine - 1), halo_copy(3, prb, halo_prb, 2, mine - 1)]

    @pl.when(has_after)
    def _():
        for copy in to_after:
            copy.start()

    @pl.when(has_before)
    def _():
        for copy in to_before:
            copy.start()

    own = [
        pltpu.make_async_copy(pts, halo_pts.at[1], own_sem.at[0]),
        pltpu.make_async_copy(prb, halo_prb.at[1], own_sem.at[1]),
    ]
    for copy in own:
        copy.start()

    def leaf_step(ids):
        done = []
        for i in ids:
            span = pl.ds(pl.multiple_of(i * leaf_len, leaf_len), leaf_len)
            tile = pts[:, span]
            pieces = half_norms(tile)
            right = norm_rows(pieces, 3)
            left_rows = norm_rows(pieces, 0)
            tile_left = deep(tile, left_rows).T
            stacked = jnp.concatenate([tile, right, left_rows], axis=0)
            node = mm(stacked, one_hot(leaf_len, leaf_skel[pl.ds(i, 1), :])).astype(BF16)
            raw = mm(tile_left, deep(node[: emb_width + PIECE]))
            high, low = split(affinity(raw, emb_width))
            tile_prb = prb[:, span]
            charge = (mm(tile_prb, high) + mm(tile_prb, low)).astype(BF16)
            done.append((span, right, tile_left, node, high, low, charge))
        for i, (span, right, tile_left, node, high, low, charge) in zip(ids, done):
            left[span, :] = tile_left
            right_rows[:, span] = right
            lk_high[span, :] = high
            lk_low[span, :] = low
            nodes[i] = node
            node_q[i] = charge

    in_groups(leaf_dev, 4, leaf_step)
    count = leaf_dev // 2
    row_base = 0
    while count:

        def level_step(ids, row_base=row_base):
            done = []
            for k in ids:
                row = row_base + k
                done.append(
                    tree_node(
                        nodes[2 * row], nodes[2 * row + 1], node_q[2 * row], node_q[2 * row + 1],
                        local_skel[pl.ds(row, 1), :], emb_width,
                    )
                )
            for k, (parent, parent_q, high, low, one, two) in zip(ids, done):
                row = row_base + k
                nodes[leaf_dev + row] = parent
                node_q[leaf_dev + row] = parent_q
                up_high[row] = high
                up_low[row] = low
                couple[2 * row] = one
                couple[2 * row + 1] = two

        in_groups(count, 4, level_step)
        row_base += count
        count //= 2
    top = 2 * leaf_dev - 2
    outbox[0, :pts_rows, :] = nodes[top]
    outbox[0, pts_rows:, :] = node_q[top]

    chunk = min(256, leaf_len)

    def own_pairs(i, carry):
        terms = []
        for k in range(PAIRS):
            leaf = i * PAIRS + k
            start = pl.multiple_of(leaf * leaf_len, leaf_len)
            span = pl.ds(start, leaf_len)
            right = deep(pts[:, span], right_rows[:, span])
            for at in range(0, leaf_len, chunk):
                part = left[pl.ds(pl.multiple_of(start + at, chunk), chunk), :]
                block = affinity(mm(part, right), emb_width).astype(BF16)
                terms.append((leaf, at, mm_nt(prb[:, span], block)))
        for leaf, at, term in terms:
            near[leaf, :, at : at + chunk] = term
        return carry

    groups = leaf_dev // PAIRS
    for level in range(levels):
        exchange = pltpu.make_async_remote_copy(
            src_ref=outbox.at[level], dst_ref=inbox.at[level],
            send_sem=box_send.at[level], recv_sem=box_recv.at[level],
            device_id=(partners[level],), device_id_type=MESH,
        )
        exchange.start()
        lax.fori_loop(level * groups // levels, (level + 1) * groups // levels, own_pairs, 0)
        exchange.wait()
        is_first = bits[level] == 0
        here = outbox[level]
        there = inbox[level]
        one = jnp.where(is_first, here, there)
        two = jnp.where(is_first, there, here)
        row = dev_num - (dev_num >> level) + lax.div(mine, 2 << level)
        parent, parent_q, high, low, couple_one, couple_two = tree_node(
            one[:pts_rows], two[:pts_rows], one[pts_rows:], two[pts_rows:],
            upper_skel[pl.ds(row, 1), :], emb_width,
        )
        path_high[level] = high
        path_low[level] = low
        path_couple[level] = jnp.where(is_first, couple_one, couple_two)
        if level < levels - 1:
            outbox[level + 1, :pts_rows, :] = parent
            outbox[level + 1, pts_rows:, :] = parent_q

    field = jnp.zeros(path_couple.shape[1:], F32)
    for level in reversed(range(levels)):
        spread = spread_down(field, path_high[level], path_low[level])
        field = jnp.where(bits[level] == 0, spread[:, :skel], spread[:, skel:]) + path_couple[level]
    fields[top] = field
    count = 1
    row_base = leaf_dev - 2
    while count < leaf_dev:

        def down_step(ids, row_base=row_base):
            done = []
            for k in ids:
                row = row_base + k
                spread = spread_down(fields[leaf_dev + row], up_high[row], up_low[row])
                done.append((spread[:, :skel] + couple[2 * row], spread[:, skel:] + couple[2 * row + 1]))
            for k, (one, two) in zip(ids, done):
                fields[2 * (row_base + k)] = one
                fields[2 * (row_base + k) + 1] = two

        in_groups(count, 4, down_step)
        count *= 2
        row_base -= count

    def far_step(ids):
        for i in ids:
            span = pl.ds(pl.multiple_of(i * leaf_len, leaf_len), leaf_len)
            far[:, span] = spread_down(fields[i], lk_high[span, :], lk_low[span, :])

    in_groups(leaf_dev, 4, far_step)
    for copy in own:
        copy.wait()

    @pl.when(has_after)
    def _():
        for copy in to_after:
            copy.wait_send()
        for copy in to_before:
            copy.wait_recv()

    @pl.when(has_before)
    def _():
        for copy in to_before:
            copy.wait_send()
        for copy in to_after:
            copy.wait_recv()


def list_pairs(near_list, near_count, base, targets, sources):
    leaf_dev = near_list.shape[0]

    def of_leaf(leaf, found):
        def of_slot(slot, found):
            targets[found] = leaf
            sources[found] = jnp.clip(near_list[leaf, slot] - base, 0, 3 * leaf_dev - 1)
            return found + 1

        return lax.fori_loop(1, near_count[leaf], of_slot, found)

    found = lax.fori_loop(0, leaf_dev, of_leaf, 0)
    for k in range(PAIRS - 1):
        targets[found + k] = leaf_dev
        sources[found + k] = leaf_dev
    return (found + PAIRS - 1) // PAIRS


def near_body(me, near_list, near_count, left, pts, prb, own, far, out, total, rows, targets, sources):
    leaf_dev = near_list.shape[0]
    leaf_len = total.shape[2]
    emb_width = pts.shape[1]
    chunk = min(256, leaf_len)
    total[:leaf_dev] = own[...]
    total[leaf_dev] = jnp.zeros(total.shape[1:], F32)
    steps = list_pairs(near_list, near_count, (me[0] - 1) * leaf_dev, targets, sources)

    def norms(ids):
        for i in ids:
            span = pl.ds(pl.multiple_of(i * leaf_len, leaf_len), leaf_len)
            for which in range(3):
                rows[which, :, span] = norm_rows(half_norms(pts[which, :, span]), 3)

    in_groups(leaf_dev, 2, norms)

    def step(i, carry):
        done = []
        for k in range(PAIRS):
            target = targets[i * PAIRS + k]
            source = sources[i * PAIRS + k]
            which = lax.div(source, leaf_dev)
            span = pl.ds(pl.multiple_of(lax.rem(source, leaf_dev) * leaf_len, leaf_len), leaf_len)
            right = deep(pts[which, :, span], rows[which, :, span])
            source_prb = prb[which, :, span]
            left_at = jnp.minimum(target, leaf_dev - 1) * leaf_len
            for at in range(0, leaf_len, chunk):
                part = left[pl.ds(pl.multiple_of(left_at + at, chunk), chunk), :]
                block = affinity(mm(part, right), emb_width).astype(BF16)
                done.append((target, at, mm_nt(source_prb, block)))
        for target, at, term in done:
            total[target, :, at : at + chunk] += term
        return carry

    lax.fori_loop(0, steps, step, 0)
    for leaf in range(leaf_dev):
        span = slice(leaf * leaf_len, (leaf + 1) * leaf_len)
        out[:, span] = total[leaf] + far[:, span]


def shape(dims, dtype):
    return jax.ShapeDtypeStruct(tuple(dims), dtype)


def per_device(points, probes, near_list, near_count, leaf_skel, local_skel, upper_skel):
    emb_width, shard_len = points.shape
    leaf_dev, slots = near_list.shape
    leaf_len = shard_len // leaf_dev
    skel = leaf_skel.shape[1]
    probe_num = probes.shape[0]
    levels = lax.axis_size("leaf").bit_length() - 1
    me = lax.axis_index("leaf").astype(jnp.int32).reshape(1)
    low_nodes = leaf_dev - 1
    all_nodes = 2 * leaf_dev - 1
    pts_rows = emb_width + 2 * PIECE
    vmem = pl.BlockSpec(memory_space=pltpu.VMEM)
    smem = pl.BlockSpec(memory_space=pltpu.SMEM)
    anywhere = pl.BlockSpec(memory_space=pl.ANY)
    left, near, far, halo_pts, halo_prb = pl.pallas_call(
        tree_body,
        out_shape=[
            shape((shard_len, DEEP), BF16),
            shape((leaf_dev, probe_num, leaf_len), F32),
            shape((probe_num, shard_len), F32),
            shape((3, emb_width, shard_len), BF16),
            shape((3, probe_num, shard_len), BF16),
        ],
        in_specs=[vmem] * 5,
        out_specs=[vmem] * 3 + [anywhere] * 2,
        scratch_shapes=[
            pltpu.VMEM((PIECE, shard_len), BF16),
            pltpu.VMEM((shard_len, skel), BF16),
            pltpu.VMEM((shard_len, skel), BF16),
            pltpu.VMEM((low_nodes, 2 * skel, skel), BF16),
            pltpu.VMEM((low_nodes, 2 * skel, skel), BF16),
            pltpu.VMEM((2 * low_nodes, probe_num, skel), F32),
            pltpu.VMEM((all_nodes, pts_rows, skel), BF16),
            pltpu.VMEM((all_nodes, probe_num, skel), BF16),
            pltpu.VMEM((levels, pts_rows + probe_num, skel), BF16),
            pltpu.VMEM((levels, pts_rows + probe_num, skel), BF16),
            pltpu.VMEM((levels, 2 * skel, skel), BF16),
            pltpu.VMEM((levels, 2 * skel, skel), BF16),
            pltpu.VMEM((levels, probe_num, skel), F32),
            pltpu.VMEM((all_nodes, probe_num, skel), F32),
            pltpu.SemaphoreType.DMA((2,)),
            pltpu.SemaphoreType.DMA((4,)),
            pltpu.SemaphoreType.DMA((4,)),
            pltpu.SemaphoreType.DMA((levels,)),
            pltpu.SemaphoreType.DMA((levels,)),
        ],
        compiler_params=pltpu.CompilerParams(
            vmem_limit_bytes=VMEM_LIMIT, collective_id=0, has_side_effects=True
        ),
        name="tree_and_halo",
    )(points, probes, leaf_skel, local_skel, upper_skel)

    pair_len = slots * leaf_dev + PAIRS
    return pl.pallas_call(
        near_body,
        out_shape=shape((probe_num, shard_len), F32),
        in_specs=[smem] * 3 + [vmem] * 5,
        out_specs=vmem,
        scratch_shapes=[
            pltpu.VMEM((leaf_dev + 1, probe_num, leaf_len), F32),
            pltpu.VMEM((3, PIECE, shard_len), BF16),
            pltpu.SMEM((pair_len,), jnp.int32),
            pltpu.SMEM((pair_len,), jnp.int32),
        ],
        compiler_params=pltpu.CompilerParams(vmem_limit_bytes=VMEM_LIMIT),
        name="near_field",
    )(me, near_list, near_count, left, halo_pts, halo_prb, near, far)


def solution(mesh):
    in_specs = (
        P(None, "leaf"),
        P(None, "leaf"),
        P("leaf", None),
        P("leaf"),
        P("leaf", None),
        P("leaf", None),
        P(),
    )
    return jax.shard_map(
        per_device, mesh=mesh, in_specs=in_specs, out_specs=P(None, "leaf"), check_vma=False
    )
```

```python
import math

import jax
import jax.numpy as jnp
from jax import lax
from jax.experimental import pallas as pl
from jax.experimental.pallas import tpu as pltpu
from jax.sharding import PartitionSpec as P

F32 = jnp.float32
BF16 = jnp.bfloat16
DEEP = 256
PIECE = 16
PAIRS = 2
VMEM_LIMIT = 56 * 1024 * 1024
MESH = pl.DeviceIdType.MESH


def mm(left, right):
    return jnp.dot(left, right, preferred_element_type=F32)


def mm_nt(left, right):
    return lax.dot_general(left, right, (((1,), (1,)), ((), ())), preferred_element_type=F32)


def split(value):
    high = value.astype(BF16)
    low = (value - high.astype(F32)).astype(BF16)
    return high, low


def affinity(scaled, emb_width):
    return jnp.exp2(scaled * (4.0 / emb_width * math.log2(math.e)))


def half_norms(pts):
    wide = pts.astype(F32)
    value = jnp.sum(wide * wide, axis=0, keepdims=True) * -0.5
    first = value.astype(BF16).astype(F32)
    rest = value - first
    second = rest.astype(BF16).astype(F32)
    third = (rest - second).astype(BF16).astype(F32)
    return first, second, third


def norm_rows(pieces, start):
    width = pieces[0].shape[1]
    row = lax.broadcasted_iota(jnp.int32, (PIECE, width), 0)
    rows = jnp.where(row < 6, 1.0, 0.0)
    for k, piece in enumerate(pieces):
        rows = jnp.where(row == start + k, piece, rows)
    return rows.astype(BF16)


def deep(*blocks):
    rows = sum(block.shape[0] for block in blocks)
    filler = jnp.zeros((DEEP - rows, blocks[0].shape[1]), BF16)
    return jnp.concatenate([*blocks, filler], axis=0)


def one_hot(pool, chosen):
    column = lax.broadcasted_iota(jnp.int32, (pool, chosen.shape[1]), 0)
    return jnp.where(column == chosen, 1.0, 0.0).astype(BF16)


def in_groups(total, size, step):
    size = min(size, total)
    if size == total:
        step(list(range(total)))
        return

    def body(i, carry):
        step([i * size + k for k in range(size)])
        return carry

    lax.fori_loop(0, total // size, body, 0)


def tree_node(first, second, first_q, second_q, chosen, emb_width):
    skel = first.shape[1]
    right_end = emb_width + PIECE
    joined = jnp.concatenate([first, second], axis=1)
    parent = mm(joined, one_hot(2 * skel, chosen)).astype(BF16)
    left = deep(joined[:emb_width], joined[right_end:]).T
    right = deep(jnp.concatenate([parent[:right_end], second[:right_end]], axis=1))
    raw = mm(left, right)
    up_high, up_low = split(affinity(raw[:, :skel], emb_width))
    joined_q = jnp.concatenate([first_q, second_q], axis=1)
    parent_q = (mm(joined_q, up_high) + mm(joined_q, up_low)).astype(BF16)
    cross_high, cross_low = split(affinity(raw[:skel, skel:], emb_width))
    couple_first = mm_nt(second_q, cross_high) + mm_nt(second_q, cross_low)
    couple_second = mm(first_q, cross_high) + mm(first_q, cross_low)
    return parent, parent_q, up_high, up_low, couple_first, couple_second


def spread_down(field, up_high, up_low):
    rows = field.shape[0]
    high, low = split(field)
    both = mm_nt(jnp.concatenate([high, low], axis=0), up_high)
    return both[:rows] + both[rows:] + mm_nt(high, up_low)


def tree_body(
    pts, prb, leaf_skel, local_skel, upper_skel,
    left, near, far, halo_pts, halo_prb,
    right_rows, lk_high, lk_low, up_high, up_low, couple, nodes, node_q,
    outbox, inbox, path_high, path_low, path_couple, fields,
    own_sem, halo_send, halo_recv, box_send, box_recv,
):
    emb_width = pts.shape[0]
    leaf_dev, skel = leaf_skel.shape
    leaf_len = pts.shape[1] // leaf_dev
    pts_rows = nodes.shape[1]
    levels = inbox.shape[0]
    dev_num = 1 << levels
    mine = lax.axis_index("leaf")
    bits = [lax.rem(lax.div(mine, 1 << level), 2) for level in range(levels)]
    partners = [mine + (1 - 2 * bits[level]) * (1 << level) for level in range(levels)]

    barrier = pltpu.get_barrier_semaphore()
    for peer in partners:
        pl.semaphore_signal(barrier, inc=1, device_id=(peer,), device_id_type=MESH)
    has_before = mine > 0
    has_after = mine < dev_num - 1
    crosses_before = jnp.logical_and(has_before, bits[0] == 0)
    crosses_after = jnp.logical_and(has_after, bits[0] == 1)

    @pl.when(crosses_before)
    def _():
        pl.semaphore_signal(barrier, inc=1, device_id=(mine - 1,), device_id_type=MESH)

    @pl.when(crosses_after)
    def _():
        pl.semaphore_signal(barrier, inc=1, device_id=(mine + 1,), device_id_type=MESH)

    pl.semaphore_wait(barrier, levels + jnp.where(jnp.logical_or(crosses_before, crosses_after), 1, 0))

    def halo_copy(which, source, target, peer):
        return pltpu.make_async_remote_copy(
            src_ref=source, dst_ref=target, send_sem=halo_send.at[which], recv_sem=halo_recv.at[which],
            device_id=(peer,), device_id_type=MESH,
        )

    def rise_piece(k):
        span = pl.ds(k * leaf_len, leaf_len)
        return halo_copy(3 + k, pts.at[:, span], halo_pts.at[0, :, span], mine + 1)

    to_before = [halo_copy(0, pts, halo_pts.at[2], mine - 1), halo_copy(1, prb, halo_prb.at[2], mine - 1)]
    to_after = [halo_copy(2, prb, halo_prb.at[0], mine + 1)] + [rise_piece(k) for k in range(leaf_dev)]
    low_levels = leaf_dev.bit_length() - 1
    phases = levels + 1 + low_levels

    def feed(phase):
        @pl.when(has_after)
        def _():
            for copy in to_after[phase * len(to_after) // phases : (phase + 1) * len(to_after) // phases]:
                copy.start()

    @pl.when(has_before)
    def _():
        for copy in to_before:
            copy.start()

    own = [
        pltpu.make_async_copy(pts, halo_pts.at[1], own_sem.at[0]),
        pltpu.make_async_copy(prb, halo_prb.at[1], own_sem.at[1]),
    ]
    for copy in own:
        copy.start()

    def leaf_step(ids):
        done = []
        for i in ids:
            span = pl.ds(pl.multiple_of(i * leaf_len, leaf_len), leaf_len)
            tile = pts[:, span]
            pieces = half_norms(tile)
            right = norm_rows(pieces, 3)
            left_rows = norm_rows(pieces, 0)
            tile_left = deep(tile, left_rows).T
            stacked = jnp.concatenate([tile, right, left_rows], axis=0)
            node = mm(stacked, one_hot(leaf_len, leaf_skel[pl.ds(i, 1), :])).astype(BF16)
            raw = mm(tile_left, deep(node[: emb_width + PIECE]))
            high, low = split(affinity(raw, emb_width))
            tile_prb = prb[:, span]
            charge = (mm(tile_prb, high) + mm(tile_prb, low)).astype(BF16)
            done.append((span, right, tile_left, node, high, low, charge))
        for i, (span, right, tile_left, node, high, low, charge) in zip(ids, done):
            left[span, :] = tile_left
            right_rows[:, span] = right
            lk_high[span, :] = high
            lk_low[span, :] = low
            nodes[i] = node
            node_q[i] = charge

    in_groups(leaf_dev, 4, leaf_step)
    count = leaf_dev // 2
    row_base = 0
    while count:

        def level_step(ids, row_base=row_base):
            done = []
            for k in ids:
                row = row_base + k
                done.append(
                    tree_node(
                        nodes[2 * row], nodes[2 * row + 1], node_q[2 * row], node_q[2 * row + 1],
                        local_skel[pl.ds(row, 1), :], emb_width,
                    )
                )
            for k, (parent, parent_q, high, low, one, two) in zip(ids, done):
                row = row_base + k
                nodes[leaf_dev + row] = parent
                node_q[leaf_dev + row] = parent_q
                up_high[row] = high
                up_low[row] = low
                couple[2 * row] = one
                couple[2 * row + 1] = two

        in_groups(count, 4, level_step)
        row_base += count
        count //= 2
    top = 2 * leaf_dev - 2
    outbox[0, :pts_rows, :] = nodes[top]
    outbox[0, pts_rows:, :] = node_q[top]

    chunk = min(256, leaf_len)

    def own_pairs(i, carry):
        terms = []
        for k in range(PAIRS):
            leaf = i * PAIRS + k
            start = pl.multiple_of(leaf * leaf_len, leaf_len)
            span = pl.ds(start, leaf_len)
            right = deep(pts[:, span], right_rows[:, span])
            for at in range(0, leaf_len, chunk):
                part = left[pl.ds(pl.multiple_of(start + at, chunk), chunk), :]
                block = affinity(mm(part, right), emb_width).astype(BF16)
                terms.append((leaf, at, mm_nt(prb[:, span], block)))
        for leaf, at, term in terms:
            near[leaf, :, at : at + chunk] = term
        return carry

    groups = leaf_dev // PAIRS
    later = groups - groups // 2
    shares = [0] + [groups // 2 + level * later // (levels - 1) for level in range(levels)]
    for level in range(levels):
        exchange = pltpu.make_async_remote_copy(
            src_ref=outbox.at[level], dst_ref=inbox.at[level],
            send_sem=box_send.at[level], recv_sem=box_recv.at[level],
            device_id=(partners[level],), device_id_type=MESH,
        )
        exchange.start()
        feed(level)
        lax.fori_loop(shares[level], shares[level + 1], own_pairs, 0)
        exchange.wait()
        is_first = bits[level] == 0
        here = outbox[level]
        there = inbox[level]
        one = jnp.where(is_first, here, there)
        two = jnp.where(is_first, there, here)
        row = dev_num - (dev_num >> level) + lax.div(mine, 2 << level)
        parent, parent_q, high, low, couple_one, couple_two = tree_node(
            one[:pts_rows], two[:pts_rows], one[pts_rows:], two[pts_rows:],
            upper_skel[pl.ds(row, 1), :], emb_width,
        )
        path_high[level] = high
        path_low[level] = low
        path_couple[level] = jnp.where(is_first, couple_one, couple_two)
        if level < levels - 1:
            outbox[level + 1, :pts_rows, :] = parent
            outbox[level + 1, pts_rows:, :] = parent_q

    feed(levels)
    field = jnp.zeros(path_couple.shape[1:], F32)
    for level in reversed(range(levels)):
        spread = spread_down(field, path_high[level], path_low[level])
        field = jnp.where(bits[level] == 0, spread[:, :skel], spread[:, skel:]) + path_couple[level]
    fields[top] = field
    count = 1
    row_base = leaf_dev - 2
    while count < leaf_dev:
        feed(levels + count.bit_length())

        def down_step(ids, row_base=row_base):
            done = []
            for k in ids:
                row = row_base + k
                spread = spread_down(fields[leaf_dev + row], up_high[row], up_low[row])
                done.append((spread[:, :skel] + couple[2 * row], spread[:, skel:] + couple[2 * row + 1]))
            for k, (one, two) in zip(ids, done):
                fields[2 * (row_base + k)] = one
                fields[2 * (row_base + k) + 1] = two

        in_groups(count, 4, down_step)
        count *= 2
        row_base -= count

    def far_step(ids):
        for i in ids:
            span = pl.ds(pl.multiple_of(i * leaf_len, leaf_len), leaf_len)
            far[:, span] = spread_down(fields[i], lk_high[span, :], lk_low[span, :])

    in_groups(leaf_dev, 4, far_step)
    for copy in own:
        copy.wait()

    @pl.when(has_after)
    def _():
        for copy in to_after:
            copy.wait_send()
        for copy in to_before:
            copy.wait_recv()

    @pl.when(has_before)
    def _():
        for copy in to_before:
            copy.wait_send()
        for copy in to_after:
            copy.wait_recv()


def list_pairs(near_list, near_count, base, targets, sources):
    leaf_dev = near_list.shape[1]

    def of_leaf(leaf, found):
        def of_slot(slot, found):
            targets[found] = leaf
            sources[found] = jnp.clip(near_list[slot, leaf] - base, 0, 3 * leaf_dev - 1)
            return found + 1

        return lax.fori_loop(1, near_count[leaf], of_slot, found)

    found = lax.fori_loop(0, leaf_dev, of_leaf, 0)
    for k in range(PAIRS - 1):
        targets[found + k] = leaf_dev
        sources[found + k] = leaf_dev
    return (found + PAIRS - 1) // PAIRS


def near_body(me, near_list, near_count, left, pts, prb, own, far, out, total, rows, targets, sources):
    leaf_dev = near_list.shape[1]
    leaf_len = total.shape[2]
    emb_width = pts.shape[1]
    chunk = min(256, leaf_len)
    total[:leaf_dev] = own[...]
    total[leaf_dev] = jnp.zeros(total.shape[1:], F32)
    steps = list_pairs(near_list, near_count, (me[0] - 1) * leaf_dev, targets, sources)

    def norms(ids):
        for i in ids:
            span = pl.ds(pl.multiple_of(i * leaf_len, leaf_len), leaf_len)
            for which in range(3):
                rows[which, :, span] = norm_rows(half_norms(pts[which, :, span]), 3)

    in_groups(leaf_dev, 2, norms)

    def step(i, carry):
        done = []
        for k in range(PAIRS):
            target = targets[i * PAIRS + k]
            source = sources[i * PAIRS + k]
            which = lax.div(source, leaf_dev)
            span = pl.ds(pl.multiple_of(lax.rem(source, leaf_dev) * leaf_len, leaf_len), leaf_len)
            right = deep(pts[which, :, span], rows[which, :, span])
            source_prb = prb[which, :, span]
            left_at = jnp.minimum(target, leaf_dev - 1) * leaf_len
            for at in range(0, leaf_len, chunk):
                part = left[pl.ds(pl.multiple_of(left_at + at, chunk), chunk), :]
                block = affinity(mm(part, right), emb_width).astype(BF16)
                done.append((target, at, mm_nt(source_prb, block)))
        for target, at, term in done:
            total[target, :, at : at + chunk] += term
        return carry

    lax.fori_loop(0, steps, step, 0)
    for leaf in range(leaf_dev):
        span = slice(leaf * leaf_len, (leaf + 1) * leaf_len)
        out[:, span] = total[leaf] + far[:, span]


def shape(dims, dtype):
    return jax.ShapeDtypeStruct(tuple(dims), dtype)


def per_device(points, probes, near_list, near_count, leaf_skel, local_skel, upper_skel):
    emb_width, shard_len = points.shape
    leaf_dev, slots = near_list.shape
    leaf_len = shard_len // leaf_dev
    skel = leaf_skel.shape[1]
    probe_num = probes.shape[0]
    levels = lax.axis_size("leaf").bit_length() - 1
    me = lax.axis_index("leaf").astype(jnp.int32).reshape(1)
    low_nodes = leaf_dev - 1
    all_nodes = 2 * leaf_dev - 1
    pts_rows = emb_width + 2 * PIECE
    vmem = pl.BlockSpec(memory_space=pltpu.VMEM)
    smem = pl.BlockSpec(memory_space=pltpu.SMEM)
    anywhere = pl.BlockSpec(memory_space=pl.ANY)
    left, near, far, halo_pts, halo_prb = pl.pallas_call(
        tree_body,
        out_shape=[
            shape((shard_len, DEEP), BF16),
            shape((leaf_dev, probe_num, leaf_len), F32),
            shape((probe_num, shard_len), F32),
            shape((3, emb_width, shard_len), BF16),
            shape((3, probe_num, shard_len), BF16),
        ],
        in_specs=[vmem] * 5,
        out_specs=[vmem] * 3 + [anywhere] * 2,
        scratch_shapes=[
            pltpu.VMEM((PIECE, shard_len), BF16),
            pltpu.VMEM((shard_len, skel), BF16),
            pltpu.VMEM((shard_len, skel), BF16),
            pltpu.VMEM((low_nodes, 2 * skel, skel), BF16),
            pltpu.VMEM((low_nodes, 2 * skel, skel), BF16),
            pltpu.VMEM((2 * low_nodes, probe_num, skel), F32),
            pltpu.VMEM((all_nodes, pts_rows, skel), BF16),
            pltpu.VMEM((all_nodes, probe_num, skel), BF16),
            pltpu.VMEM((levels, pts_rows + probe_num, skel), BF16),
            pltpu.VMEM((levels, pts_rows + probe_num, skel), BF16),
            pltpu.VMEM((levels, 2 * skel, skel), BF16),
            pltpu.VMEM((levels, 2 * skel, skel), BF16),
            pltpu.VMEM((levels, probe_num, skel), F32),
            pltpu.VMEM((all_nodes, probe_num, skel), F32),
            pltpu.SemaphoreType.DMA((2,)),
            pltpu.SemaphoreType.DMA((3 + leaf_dev,)),
            pltpu.SemaphoreType.DMA((3 + leaf_dev,)),
            pltpu.SemaphoreType.DMA((levels,)),
            pltpu.SemaphoreType.DMA((levels,)),
        ],
        compiler_params=pltpu.CompilerParams(
            vmem_limit_bytes=VMEM_LIMIT, collective_id=0, has_side_effects=True
        ),
        name="tree_and_halo",
    )(points, probes, leaf_skel, local_skel, upper_skel)

    pair_len = slots * leaf_dev + PAIRS
    return pl.pallas_call(
        near_body,
        out_shape=shape((probe_num, shard_len), F32),
        in_specs=[smem] * 3 + [vmem] * 5,
        out_specs=vmem,
        scratch_shapes=[
            pltpu.VMEM((leaf_dev + 1, probe_num, leaf_len), F32),
            pltpu.VMEM((3, PIECE, shard_len), BF16),
            pltpu.SMEM((pair_len,), jnp.int32),
            pltpu.SMEM((pair_len,), jnp.int32),
        ],
        compiler_params=pltpu.CompilerParams(vmem_limit_bytes=VMEM_LIMIT),
        name="near_field",
    )(me, near_list.T, near_count, left, halo_pts, halo_prb, near, far)


def solution(mesh):
    in_specs = (
        P(None, "leaf"),
        P(None, "leaf"),
        P("leaf", None),
        P("leaf"),
        P("leaf", None),
        P("leaf", None),
        P(),
    )
    return jax.shard_map(
        per_device, mesh=mesh, in_specs=in_specs, out_specs=P(None, "leaf"), check_vma=False
    )
```

```python
import math

import jax
import jax.numpy as jnp
from jax import lax
from jax.experimental import pallas as pl
from jax.experimental.pallas import tpu as pltpu
from jax.sharding import PartitionSpec as P

F32 = jnp.float32
BF16 = jnp.bfloat16
DEEP = 256
PIECE = 16
PAIRS = 2
VMEM_LIMIT = 56 * 1024 * 1024
MESH = pl.DeviceIdType.MESH


def mm(left, right):
    return jnp.dot(left, right, preferred_element_type=F32)


def mm_nt(left, right):
    return lax.dot_general(left, right, (((1,), (1,)), ((), ())), preferred_element_type=F32)


def split(value):
    high = value.astype(BF16)
    low = (value - high.astype(F32)).astype(BF16)
    return high, low


def affinity(scaled, emb_width):
    return jnp.exp2(scaled * (4.0 / emb_width * math.log2(math.e)))


def half_norms(pts):
    wide = pts.astype(F32)
    value = jnp.sum(wide * wide, axis=0, keepdims=True) * -0.5
    first = value.astype(BF16).astype(F32)
    rest = value - first
    second = rest.astype(BF16).astype(F32)
    third = (rest - second).astype(BF16).astype(F32)
    return first, second, third


def norm_rows(pieces, start):
    width = pieces[0].shape[1]
    row = lax.broadcasted_iota(jnp.int32, (PIECE, width), 0)
    rows = jnp.where(row < 6, 1.0, 0.0)
    for k, piece in enumerate(pieces):
        rows = jnp.where(row == start + k, piece, rows)
    return rows.astype(BF16)


def deep(*blocks):
    rows = sum(block.shape[0] for block in blocks)
    filler = jnp.zeros((DEEP - rows, blocks[0].shape[1]), BF16)
    return jnp.concatenate([*blocks, filler], axis=0)


def one_hot(pool, chosen):
    column = lax.broadcasted_iota(jnp.int32, (pool, chosen.shape[1]), 0)
    return jnp.where(column == chosen, 1.0, 0.0).astype(BF16)


def in_groups(total, size, step):
    size = min(size, total)
    if size == total:
        step(list(range(total)))
        return

    def body(i, carry):
        step([i * size + k for k in range(size)])
        return carry

    lax.fori_loop(0, total // size, body, 0)


def tree_node(first, second, first_q, second_q, chosen, emb_width):
    skel = first.shape[1]
    right_end = emb_width + PIECE
    joined = jnp.concatenate([first, second], axis=1)
    parent = mm(joined, one_hot(2 * skel, chosen)).astype(BF16)
    left = deep(joined[:emb_width], joined[right_end:]).T
    right = deep(jnp.concatenate([parent[:right_end], second[:right_end]], axis=1))
    raw = mm(left, right)
    up_high, up_low = split(affinity(raw[:, :skel], emb_width))
    joined_q = jnp.concatenate([first_q, second_q], axis=1)
    parent_q = (mm(joined_q, up_high) + mm(joined_q, up_low)).astype(BF16)
    cross_high, cross_low = split(affinity(raw[:skel, skel:], emb_width))
    couple_first = mm_nt(second_q, cross_high) + mm_nt(second_q, cross_low)
    couple_second = mm(first_q, cross_high) + mm(first_q, cross_low)
    return parent, parent_q, up_high, up_low, couple_first, couple_second


def spread_down(field, up_high, up_low):
    rows = field.shape[0]
    high, low = split(field)
    both = mm_nt(jnp.concatenate([high, low], axis=0), up_high)
    return both[:rows] + both[rows:] + mm_nt(high, up_low)


def tree_body(
    pts, prb, leaf_skel, local_skel, upper_skel,
    left, near, far, halo_pts, halo_prb,
    right_rows, lk_high, lk_low, up_high, up_low, couple, nodes, node_q,
    outbox, inbox, path_high, path_low, path_couple, fields,
    own_sem, halo_send, halo_recv, box_send, box_recv,
):
    emb_width = pts.shape[0]
    leaf_dev, skel = leaf_skel.shape
    leaf_len = pts.shape[1] // leaf_dev
    pts_rows = nodes.shape[1]
    levels = inbox.shape[0]
    dev_num = 1 << levels
    mine = lax.axis_index("leaf")
    bits = [lax.rem(lax.div(mine, 1 << level), 2) for level in range(levels)]
    partners = [mine + (1 - 2 * bits[level]) * (1 << level) for level in range(levels)]

    barrier = pltpu.get_barrier_semaphore()
    for peer in partners:
        pl.semaphore_signal(barrier, inc=1, device_id=(peer,), device_id_type=MESH)
    has_before = mine > 0
    has_after = mine < dev_num - 1
    crosses_before = jnp.logical_and(has_before, bits[0] == 0)
    crosses_after = jnp.logical_and(has_after, bits[0] == 1)

    @pl.when(crosses_before)
    def _():
        pl.semaphore_signal(barrier, inc=1, device_id=(mine - 1,), device_id_type=MESH)

    @pl.when(crosses_after)
    def _():
        pl.semaphore_signal(barrier, inc=1, device_id=(mine + 1,), device_id_type=MESH)

    pl.semaphore_wait(barrier, levels + jnp.where(jnp.logical_or(crosses_before, crosses_after), 1, 0))

    def halo_copy(which, source, target, peer):
        return pltpu.make_async_remote_copy(
            src_ref=source, dst_ref=target, send_sem=halo_send.at[which], recv_sem=halo_recv.at[which],
            device_id=(peer,), device_id_type=MESH,
        )

    def flow(first_sem, slot, peer):
        copies = [halo_copy(first_sem, prb, halo_prb.at[slot], peer)]
        for k in range(leaf_dev):
            span = pl.ds(k * leaf_len, leaf_len)
            copies.append(halo_copy(first_sem + 1 + k, pts.at[:, span], halo_pts.at[slot, :, span], peer))
        return copies

    to_after = flow(0, 0, mine + 1)
    to_before = flow(1 + leaf_dev, 2, mine - 1)
    late_after = jnp.logical_and(bits[0] == 1, bits[1] == 0)
    late_before = jnp.logical_and(bits[0] == 0, bits[1] == 1)
    low_levels = leaf_dev.bit_length() - 1
    phases = levels + 1 + low_levels

    def start_when(condition, copies):
        @pl.when(condition)
        def _():
            for copy in copies:
                copy.start()

    def feed(phase):
        part = slice(phase * len(to_after) // phases, (phase + 1) * len(to_after) // phases)
        start_when(late_after, to_after[part])
        start_when(late_before, to_before[part])

    start_when(jnp.logical_and(has_after, jnp.logical_not(late_after)), to_after)
    start_when(jnp.logical_and(has_before, jnp.logical_not(late_before)), to_before)
    own = [
        pltpu.make_async_copy(pts, halo_pts.at[1], own_sem.at[0]),
        pltpu.make_async_copy(prb, halo_prb.at[1], own_sem.at[1]),
    ]
    for copy in own:
        copy.start()

    def leaf_step(ids):
        done = []
        for i in ids:
            span = pl.ds(pl.multiple_of(i * leaf_len, leaf_len), leaf_len)
            tile = pts[:, span]
            pieces = half_norms(tile)
            right = norm_rows(pieces, 3)
            left_rows = norm_rows(pieces, 0)
            tile_left = deep(tile, left_rows).T
            stacked = jnp.concatenate([tile, right, left_rows], axis=0)
            node = mm(stacked, one_hot(leaf_len, leaf_skel[pl.ds(i, 1), :])).astype(BF16)
            raw = mm(tile_left, deep(node[: emb_width + PIECE]))
            high, low = split(affinity(raw, emb_width))
            tile_prb = prb[:, span]
            charge = (mm(tile_prb, high) + mm(tile_prb, low)).astype(BF16)
            done.append((span, right, tile_left, node, high, low, charge))
        for i, (span, right, tile_left, node, high, low, charge) in zip(ids, done):
            left[span, :] = tile_left
            right_rows[:, span] = right
            lk_high[span, :] = high
            lk_low[span, :] = low
            nodes[i] = node
            node_q[i] = charge

    in_groups(leaf_dev, 4, leaf_step)
    count = leaf_dev // 2
    row_base = 0
    while count:

        def level_step(ids, row_base=row_base):
            done = []
            for k in ids:
                row = row_base + k
                done.append(
                    tree_node(
                        nodes[2 * row], nodes[2 * row + 1], node_q[2 * row], node_q[2 * row + 1],
                        local_skel[pl.ds(row, 1), :], emb_width,
                    )
                )
            for k, (parent, parent_q, high, low, one, two) in zip(ids, done):
                row = row_base + k
                nodes[leaf_dev + row] = parent
                node_q[leaf_dev + row] = parent_q
                up_high[row] = high
                up_low[row] = low
                couple[2 * row] = one
                couple[2 * row + 1] = two

        in_groups(count, 4, level_step)
        row_base += count
        count //= 2
    top = 2 * leaf_dev - 2
    outbox[0, :pts_rows, :] = nodes[top]
    outbox[0, pts_rows:, :] = node_q[top]

    chunk = min(256, leaf_len)

    def own_pairs(i, carry):
        terms = []
        for k in range(PAIRS):
            leaf = i * PAIRS + k
            start = pl.multiple_of(leaf * leaf_len, leaf_len)
            span = pl.ds(start, leaf_len)
            right = deep(pts[:, span], right_rows[:, span])
            for at in range(0, leaf_len, chunk):
                part = left[pl.ds(pl.multiple_of(start + at, chunk), chunk), :]
                block = affinity(mm(part, right), emb_width).astype(BF16)
                terms.append((leaf, at, mm_nt(prb[:, span], block)))
        for leaf, at, term in terms:
            near[leaf, :, at : at + chunk] = term
        return carry

    groups = leaf_dev // PAIRS
    later = groups - groups // 2
    shares = [0] + [groups // 2 + level * later // (levels - 1) for level in range(levels)]
    for level in range(levels):
        exchange = pltpu.make_async_remote_copy(
            src_ref=outbox.at[level], dst_ref=inbox.at[level],
            send_sem=box_send.at[level], recv_sem=box_recv.at[level],
            device_id=(partners[level],), device_id_type=MESH,
        )
        exchange.start()
        feed(level)
        lax.fori_loop(shares[level], shares[level + 1], own_pairs, 0)
        exchange.wait()
        is_first = bits[level] == 0
        here = outbox[level]
        there = inbox[level]
        one = jnp.where(is_first, here, there)
        two = jnp.where(is_first, there, here)
        row = dev_num - (dev_num >> level) + lax.div(mine, 2 << level)
        parent, parent_q, high, low, couple_one, couple_two = tree_node(
            one[:pts_rows], two[:pts_rows], one[pts_rows:], two[pts_rows:],
            upper_skel[pl.ds(row, 1), :], emb_width,
        )
        path_high[level] = high
        path_low[level] = low
        path_couple[level] = jnp.where(is_first, couple_one, couple_two)
        if level < levels - 1:
            outbox[level + 1, :pts_rows, :] = parent
            outbox[level + 1, pts_rows:, :] = parent_q

    feed(levels)
    field = jnp.zeros(path_couple.shape[1:], F32)
    for level in reversed(range(levels)):
        spread = spread_down(field, path_high[level], path_low[level])
        field = jnp.where(bits[level] == 0, spread[:, :skel], spread[:, skel:]) + path_couple[level]
    fields[top] = field
    count = 1
    row_base = leaf_dev - 2
    while count < leaf_dev:
        feed(levels + count.bit_length())

        def down_step(ids, row_base=row_base):
            done = []
            for k in ids:
                row = row_base + k
                spread = spread_down(fields[leaf_dev + row], up_high[row], up_low[row])
                done.append((spread[:, :skel] + couple[2 * row], spread[:, skel:] + couple[2 * row + 1]))
            for k, (one, two) in zip(ids, done):
                fields[2 * (row_base + k)] = one
                fields[2 * (row_base + k) + 1] = two

        in_groups(count, 4, down_step)
        count *= 2
        row_base -= count

    def far_step(ids):
        for i in ids:
            span = pl.ds(pl.multiple_of(i * leaf_len, leaf_len), leaf_len)
            far[:, span] = spread_down(fields[i], lk_high[span, :], lk_low[span, :])

    in_groups(leaf_dev, 4, far_step)
    for copy in own:
        copy.wait()

    @pl.when(has_after)
    def _():
        for copy in to_after:
            copy.wait_send()
        for copy in to_before:
            copy.wait_recv()

    @pl.when(has_before)
    def _():
        for copy in to_before:
            copy.wait_send()
        for copy in to_after:
            copy.wait_recv()


def list_pairs(near_list, near_count, base, targets, sources):
    leaf_dev = near_list.shape[1]

    def of_leaf(leaf, found):
        def of_slot(slot, found):
            targets[found] = leaf
            sources[found] = jnp.clip(near_list[slot, leaf] - base, 0, 3 * leaf_dev - 1)
            return found + 1

        return lax.fori_loop(1, near_count[leaf], of_slot, found)

    found = lax.fori_loop(0, leaf_dev, of_leaf, 0)
    for k in range(PAIRS - 1):
        targets[found + k] = leaf_dev
        sources[found + k] = leaf_dev
    return (found + PAIRS - 1) // PAIRS


def near_body(
    me, near_list, near_count, left_in, pts_in, prb_in, own, far, out,
    left, pts, prb, total, rows, targets, sources, sems,
):
    leaf_dev = near_list.shape[1]
    leaf_len = total.shape[2]
    emb_width = pts.shape[1]
    chunk = min(256, leaf_len)
    pts_copies = [pltpu.make_async_copy(pts_in.at[k], pts.at[k], sems.at[k]) for k in range(3)]
    prb_copy = pltpu.make_async_copy(prb_in, prb, sems.at[3])
    left_copy = pltpu.make_async_copy(left_in, left, sems.at[4])
    for copy in [*pts_copies, prb_copy, left_copy]:
        copy.start()
    total[:leaf_dev] = own[...]
    total[leaf_dev] = jnp.zeros(total.shape[1:], F32)
    steps = list_pairs(near_list, near_count, (me[0] - 1) * leaf_dev, targets, sources)

    for which in range(3):
        pts_copies[which].wait()

        def norms(ids, which=which):
            for i in ids:
                span = pl.ds(pl.multiple_of(i * leaf_len, leaf_len), leaf_len)
                rows[which, :, span] = norm_rows(half_norms(pts[which, :, span]), 3)

        in_groups(leaf_dev, 4, norms)
    prb_copy.wait()
    left_copy.wait()

    def step(i, carry):
        done = []
        for k in range(PAIRS):
            target = targets[i * PAIRS + k]
            source = sources[i * PAIRS + k]
            which = lax.div(source, leaf_dev)
            span = pl.ds(pl.multiple_of(lax.rem(source, leaf_dev) * leaf_len, leaf_len), leaf_len)
            right = deep(pts[which, :, span], rows[which, :, span])
            source_prb = prb[which, :, span]
            left_at = jnp.minimum(target, leaf_dev - 1) * leaf_len
            for at in range(0, leaf_len, chunk):
                part = left[pl.ds(pl.multiple_of(left_at + at, chunk), chunk), :]
                block = affinity(mm(part, right), emb_width).astype(BF16)
                done.append((target, at, mm_nt(source_prb, block)))
        for target, at, term in done:
            total[target, :, at : at + chunk] += term
        return carry

    lax.fori_loop(0, steps, step, 0)
    for leaf in range(leaf_dev):
        span = slice(leaf * leaf_len, (leaf + 1) * leaf_len)
        out[:, span] = total[leaf] + far[:, span]


def shape(dims, dtype):
    return jax.ShapeDtypeStruct(tuple(dims), dtype)


def per_device(points, probes, near_list, near_count, leaf_skel, local_skel, upper_skel):
    emb_width, shard_len = points.shape
    leaf_dev, slots = near_list.shape
    leaf_len = shard_len // leaf_dev
    skel = leaf_skel.shape[1]
    probe_num = probes.shape[0]
    levels = lax.axis_size("leaf").bit_length() - 1
    me = lax.axis_index("leaf").astype(jnp.int32).reshape(1)
    low_nodes = leaf_dev - 1
    all_nodes = 2 * leaf_dev - 1
    pts_rows = emb_width + 2 * PIECE
    vmem = pl.BlockSpec(memory_space=pltpu.VMEM)
    smem = pl.BlockSpec(memory_space=pltpu.SMEM)
    anywhere = pl.BlockSpec(memory_space=pl.ANY)
    left, near, far, halo_pts, halo_prb = pl.pallas_call(
        tree_body,
        out_shape=[
            shape((shard_len, DEEP), BF16),
            shape((leaf_dev, probe_num, leaf_len), F32),
            shape((probe_num, shard_len), F32),
            shape((3, emb_width, shard_len), BF16),
            shape((3, probe_num, shard_len), BF16),
        ],
        in_specs=[vmem] * 5,
        out_specs=[vmem] * 3 + [anywhere] * 2,
        scratch_shapes=[
            pltpu.VMEM((PIECE, shard_len), BF16),
            pltpu.VMEM((shard_len, skel), BF16),
            pltpu.VMEM((shard_len, skel), BF16),
            pltpu.VMEM((low_nodes, 2 * skel, skel), BF16),
            pltpu.VMEM((low_nodes, 2 * skel, skel), BF16),
            pltpu.VMEM((2 * low_nodes, probe_num, skel), F32),
            pltpu.VMEM((all_nodes, pts_rows, skel), BF16),
            pltpu.VMEM((all_nodes, probe_num, skel), BF16),
            pltpu.VMEM((levels, pts_rows + probe_num, skel), BF16),
            pltpu.VMEM((levels, pts_rows + probe_num, skel), BF16),
            pltpu.VMEM((levels, 2 * skel, skel), BF16),
            pltpu.VMEM((levels, 2 * skel, skel), BF16),
            pltpu.VMEM((levels, probe_num, skel), F32),
            pltpu.VMEM((all_nodes, probe_num, skel), F32),
            pltpu.SemaphoreType.DMA((2,)),
            pltpu.SemaphoreType.DMA((2 + 2 * leaf_dev,)),
            pltpu.SemaphoreType.DMA((2 + 2 * leaf_dev,)),
            pltpu.SemaphoreType.DMA((levels,)),
            pltpu.SemaphoreType.DMA((levels,)),
        ],
        compiler_params=pltpu.CompilerParams(
            vmem_limit_bytes=VMEM_LIMIT, collective_id=0, has_side_effects=True
        ),
        name="tree_and_halo",
    )(points, probes, leaf_skel, local_skel, upper_skel)

    pair_len = slots * leaf_dev + PAIRS
    return pl.pallas_call(
        near_body,
        out_shape=shape((probe_num, shard_len), F32),
        in_specs=[smem] * 3 + [anywhere] * 3 + [vmem] * 2,
        out_specs=vmem,
        scratch_shapes=[
            pltpu.VMEM((shard_len, DEEP), BF16),
            pltpu.VMEM((3, emb_width, shard_len), BF16),
            pltpu.VMEM((3, probe_num, shard_len), BF16),
            pltpu.VMEM((leaf_dev + 1, probe_num, leaf_len), F32),
            pltpu.VMEM((3, PIECE, shard_len), BF16),
            pltpu.SMEM((pair_len,), jnp.int32),
            pltpu.SMEM((pair_len,), jnp.int32),
            pltpu.SemaphoreType.DMA((5,)),
        ],
        compiler_params=pltpu.CompilerParams(vmem_limit_bytes=VMEM_LIMIT),
        name="near_field",
    )(me, near_list.T, near_count, left, halo_pts, halo_prb, near, far)


def solution(mesh):
    in_specs = (
        P(None, "leaf"),
        P(None, "leaf"),
        P("leaf", None),
        P("leaf"),
        P("leaf", None),
        P("leaf", None),
        P(),
    )
    return jax.shard_map(
        per_device, mesh=mesh, in_specs=in_specs, out_specs=P(None, "leaf"), check_vma=False
    )
```

```python
import jax
import jax.numpy as jnp
from jax import lax
from jax.experimental import pallas as pl
from jax.experimental.pallas import tpu as pltpu
from jax.sharding import PartitionSpec as P

F32 = jnp.float32
BF16 = jnp.bfloat16
DEEP = 256
PIECE = 16
PAIRS = 2
VMEM_LIMIT = 56 * 1024 * 1024
MESH = pl.DeviceIdType.MESH


def mm(left, right):
    return jnp.dot(left, right, preferred_element_type=F32)


def mm_nt(left, right):
    return lax.dot_general(left, right, (((1,), (1,)), ((), ())), preferred_element_type=F32)


def split(value):
    high = value.astype(BF16)
    low = (value - high.astype(F32)).astype(BF16)
    return high, low


def left_form(*blocks):
    return (deep(*blocks) * jnp.asarray(4.0 / blocks[0].shape[0], BF16)).T


def half_norms(pts):
    wide = pts.astype(F32)
    value = jnp.sum(wide * wide, axis=0, keepdims=True) * -0.5
    first = value.astype(BF16).astype(F32)
    rest = value - first
    second = rest.astype(BF16).astype(F32)
    third = (rest - second).astype(BF16).astype(F32)
    return first, second, third


def norm_rows(pieces, start):
    width = pieces[0].shape[1]
    row = lax.broadcasted_iota(jnp.int32, (PIECE, width), 0)
    rows = jnp.where(row < 6, 1.0, 0.0)
    for k, piece in enumerate(pieces):
        rows = jnp.where(row == start + k, piece, rows)
    return rows.astype(BF16)


def deep(*blocks):
    rows = sum(block.shape[0] for block in blocks)
    filler = jnp.zeros((DEEP - rows, blocks[0].shape[1]), BF16)
    return jnp.concatenate([*blocks, filler], axis=0)


def one_hot(pool, chosen):
    column = lax.broadcasted_iota(jnp.int32, (pool, chosen.shape[1]), 0)
    return jnp.where(column == chosen, 1.0, 0.0).astype(BF16)


def in_groups(total, size, step):
    size = min(size, total)
    if size == total:
        step(list(range(total)))
        return

    def body(i, carry):
        step([i * size + k for k in range(size)])
        return carry

    lax.fori_loop(0, total // size, body, 0)


def tree_node(first, second, first_q, second_q, chosen, emb_width):
    skel = first.shape[1]
    right_end = emb_width + PIECE
    joined = jnp.concatenate([first, second], axis=1)
    parent = mm(joined, one_hot(2 * skel, chosen)).astype(BF16)
    left = left_form(joined[:emb_width], joined[right_end:])
    right = deep(jnp.concatenate([parent[:right_end], second[:right_end]], axis=1))
    raw = mm(left, right)
    up_high, up_low = split(jnp.exp(raw[:, :skel]))
    joined_q = jnp.concatenate([first_q, second_q], axis=1)
    parent_q = (mm(joined_q, up_high) + mm(joined_q, up_low)).astype(BF16)
    cross_high, cross_low = split(jnp.exp(raw[:skel, skel:]))
    couple_first = mm_nt(second_q, cross_high) + mm_nt(second_q, cross_low)
    couple_second = mm(first_q, cross_high) + mm(first_q, cross_low)
    return parent, parent_q, up_high, up_low, couple_first, couple_second


def spread_down(field, up_high, up_low):
    rows = field.shape[0]
    high, low = split(field)
    both = mm_nt(jnp.concatenate([high, low], axis=0), up_high)
    return both[:rows] + both[rows:] + mm_nt(high, up_low)


def tree_body(
    pts, prb, leaf_skel, local_skel, upper_skel,
    left, near, far, halo_pts, halo_prb,
    right_rows, lk_high, lk_low, up_high, up_low, couple, nodes, node_q,
    outbox, inbox, path_high, path_low, path_couple, fields,
    own_sem, halo_send, halo_recv, box_send, box_recv,
):
    emb_width = pts.shape[0]
    leaf_dev, skel = leaf_skel.shape
    leaf_len = pts.shape[1] // leaf_dev
    pts_rows = nodes.shape[1]
    levels = inbox.shape[0]
    dev_num = 1 << levels
    mine = lax.axis_index("leaf")
    bits = [lax.rem(lax.div(mine, 1 << level), 2) for level in range(levels)]
    partners = [mine + (1 - 2 * bits[level]) * (1 << level) for level in range(levels)]

    barrier = pltpu.get_barrier_semaphore()
    for peer in partners:
        pl.semaphore_signal(barrier, inc=1, device_id=(peer,), device_id_type=MESH)
    has_before = mine > 0
    has_after = mine < dev_num - 1
    crosses_before = jnp.logical_and(has_before, bits[0] == 0)
    crosses_after = jnp.logical_and(has_after, bits[0] == 1)

    @pl.when(crosses_before)
    def _():
        pl.semaphore_signal(barrier, inc=1, device_id=(mine - 1,), device_id_type=MESH)

    @pl.when(crosses_after)
    def _():
        pl.semaphore_signal(barrier, inc=1, device_id=(mine + 1,), device_id_type=MESH)

    pl.semaphore_wait(barrier, levels + jnp.where(jnp.logical_or(crosses_before, crosses_after), 1, 0))

    def halo_copy(which, source, target, peer):
        return pltpu.make_async_remote_copy(
            src_ref=source, dst_ref=target, send_sem=halo_send.at[which], recv_sem=halo_recv.at[which],
            device_id=(peer,), device_id_type=MESH,
        )

    def flow(first_sem, slot, peer):
        copies = [halo_copy(first_sem, prb, halo_prb.at[slot], peer)]
        for k in range(leaf_dev):
            span = pl.ds(k * leaf_len, leaf_len)
            copies.append(halo_copy(first_sem + 1 + k, pts.at[:, span], halo_pts.at[slot, :, span], peer))
        return copies

    to_after = flow(0, 0, mine + 1)
    to_before = flow(1 + leaf_dev, 2, mine - 1)
    late_after = jnp.logical_and(bits[0] == 1, bits[1] == 0)
    late_before = jnp.logical_and(bits[0] == 0, bits[1] == 1)

    def start_when(condition, copies):
        @pl.when(condition)
        def _():
            for copy in copies:
                copy.start()

    def feed(level):
        part = slice(level * len(to_after) // levels, (level + 1) * len(to_after) // levels)
        start_when(late_after, to_after[part])
        start_when(late_before, to_before[part])

    start_when(jnp.logical_and(has_after, jnp.logical_not(late_after)), to_after)
    start_when(jnp.logical_and(has_before, jnp.logical_not(late_before)), to_before)
    own = [
        pltpu.make_async_copy(pts, halo_pts.at[1], own_sem.at[0]),
        pltpu.make_async_copy(prb, halo_prb.at[1], own_sem.at[1]),
    ]
    for copy in own:
        copy.start()

    def leaf_step(ids):
        done = []
        for i in ids:
            span = pl.ds(pl.multiple_of(i * leaf_len, leaf_len), leaf_len)
            tile = pts[:, span]
            pieces = half_norms(tile)
            right = norm_rows(pieces, 3)
            left_rows = norm_rows(pieces, 0)
            tile_left = left_form(tile, left_rows)
            stacked = jnp.concatenate([tile, right, left_rows], axis=0)
            node = mm(stacked, one_hot(leaf_len, leaf_skel[pl.ds(i, 1), :])).astype(BF16)
            raw = mm(tile_left, deep(node[: emb_width + PIECE]))
            high, low = split(jnp.exp(raw))
            tile_prb = prb[:, span]
            charge = (mm(tile_prb, high) + mm(tile_prb, low)).astype(BF16)
            done.append((span, right, tile_left, node, high, low, charge))
        for i, (span, right, tile_left, node, high, low, charge) in zip(ids, done):
            left[span, :] = tile_left
            right_rows[:, span] = right
            lk_high[span, :] = high
            lk_low[span, :] = low
            nodes[i] = node
            node_q[i] = charge

    in_groups(leaf_dev, 4, leaf_step)
    count = leaf_dev // 2
    row_base = 0
    while count:

        def level_step(ids, row_base=row_base):
            done = []
            for k in ids:
                row = row_base + k
                done.append(
                    tree_node(
                        nodes[2 * row], nodes[2 * row + 1], node_q[2 * row], node_q[2 * row + 1],
                        local_skel[pl.ds(row, 1), :], emb_width,
                    )
                )
            for k, (parent, parent_q, high, low, one, two) in zip(ids, done):
                row = row_base + k
                nodes[leaf_dev + row] = parent
                node_q[leaf_dev + row] = parent_q
                up_high[row] = high
                up_low[row] = low
                couple[2 * row] = one
                couple[2 * row + 1] = two

        in_groups(count, 4, level_step)
        row_base += count
        count //= 2
    top = 2 * leaf_dev - 2
    outbox[0, :pts_rows, :] = nodes[top]
    outbox[0, pts_rows:, :] = node_q[top]

    chunk = min(256, leaf_len)

    def own_pairs(i, carry):
        terms = []
        for k in range(PAIRS):
            leaf = i * PAIRS + k
            start = pl.multiple_of(leaf * leaf_len, leaf_len)
            span = pl.ds(start, leaf_len)
            right = deep(pts[:, span], right_rows[:, span])
            for at in range(0, leaf_len, chunk):
                part = left[pl.ds(pl.multiple_of(start + at, chunk), chunk), :]
                block = jnp.exp(mm(part, right)).astype(BF16)
                terms.append((leaf, at, mm_nt(prb[:, span], block)))
        for leaf, at, term in terms:
            near[leaf, :, at : at + chunk] = term
        return carry

    groups = leaf_dev // PAIRS
    later = groups - groups // 2
    shares = [0] + [groups // 2 + level * later // (levels - 1) for level in range(levels)]
    for level in range(levels):
        exchange = pltpu.make_async_remote_copy(
            src_ref=outbox.at[level], dst_ref=inbox.at[level],
            send_sem=box_send.at[level], recv_sem=box_recv.at[level],
            device_id=(partners[level],), device_id_type=MESH,
        )
        exchange.start()
        feed(level)
        lax.fori_loop(shares[level], shares[level + 1], own_pairs, 0)
        exchange.wait()
        is_first = bits[level] == 0
        here = outbox[level]
        there = inbox[level]
        one = jnp.where(is_first, here, there)
        two = jnp.where(is_first, there, here)
        row = dev_num - (dev_num >> level) + lax.div(mine, 2 << level)
        parent, parent_q, high, low, couple_one, couple_two = tree_node(
            one[:pts_rows], two[:pts_rows], one[pts_rows:], two[pts_rows:],
            upper_skel[pl.ds(row, 1), :], emb_width,
        )
        path_high[level] = high
        path_low[level] = low
        path_couple[level] = jnp.where(is_first, couple_one, couple_two)
        if level < levels - 1:
            outbox[level + 1, :pts_rows, :] = parent
            outbox[level + 1, pts_rows:, :] = parent_q

    field = jnp.zeros(path_couple.shape[1:], F32)
    for level in reversed(range(levels)):
        spread = spread_down(field, path_high[level], path_low[level])
        field = jnp.where(bits[level] == 0, spread[:, :skel], spread[:, skel:]) + path_couple[level]
    fields[top] = field
    count = 1
    row_base = leaf_dev - 2
    while count < leaf_dev:

        def down_step(ids, row_base=row_base):
            done = []
            for k in ids:
                row = row_base + k
                spread = spread_down(fields[leaf_dev + row], up_high[row], up_low[row])
                done.append((spread[:, :skel] + couple[2 * row], spread[:, skel:] + couple[2 * row + 1]))
            for k, (one, two) in zip(ids, done):
                fields[2 * (row_base + k)] = one
                fields[2 * (row_base + k) + 1] = two

        in_groups(count, 4, down_step)
        count *= 2
        row_base -= count

    def far_step(ids):
        for i in ids:
            span = pl.ds(pl.multiple_of(i * leaf_len, leaf_len), leaf_len)
            far[:, span] = spread_down(fields[i], lk_high[span, :], lk_low[span, :])

    in_groups(leaf_dev, 4, far_step)
    for copy in own:
        copy.wait()

    @pl.when(has_after)
    def _():
        for copy in to_after:
            copy.wait_send()
        for copy in to_before:
            copy.wait_recv()

    @pl.when(has_before)
    def _():
        for copy in to_before:
            copy.wait_send()
        for copy in to_after:
            copy.wait_recv()


def list_pairs(near_list, near_count, base, targets, sources):
    leaf_dev = near_list.shape[1]

    def of_leaf(leaf, found):
        def of_slot(slot, found):
            targets[found] = leaf
            sources[found] = jnp.clip(near_list[slot, leaf] - base, 0, 3 * leaf_dev - 1)
            return found + 1

        return lax.fori_loop(1, near_count[leaf], of_slot, found)

    found = lax.fori_loop(0, leaf_dev, of_leaf, 0)
    for k in range(PAIRS - 1):
        targets[found + k] = leaf_dev
        sources[found + k] = leaf_dev
    return (found + PAIRS - 1) // PAIRS


def near_body(
    me, near_list, near_count, left_in, pts_in, prb_in, own, far, out,
    left, pts, prb, total, rows, targets, sources, sems,
):
    leaf_dev = near_list.shape[1]
    leaf_len = total.shape[2]
    emb_width = pts.shape[1]
    chunk = min(256, leaf_len)
    pts_copies = [pltpu.make_async_copy(pts_in.at[k], pts.at[k], sems.at[k]) for k in range(3)]
    prb_copy = pltpu.make_async_copy(prb_in, prb, sems.at[3])
    left_copy = pltpu.make_async_copy(left_in, left, sems.at[4])
    for copy in [*pts_copies, prb_copy, left_copy]:
        copy.start()
    total[:leaf_dev] = own[...]
    total[leaf_dev] = jnp.zeros(total.shape[1:], F32)
    steps = list_pairs(near_list, near_count, (me[0] - 1) * leaf_dev, targets, sources)

    for which in range(3):
        pts_copies[which].wait()

        def norms(ids, which=which):
            for i in ids:
                span = pl.ds(pl.multiple_of(i * leaf_len, leaf_len), leaf_len)
                rows[which, :, span] = norm_rows(half_norms(pts[which, :, span]), 3)

        in_groups(leaf_dev, 4, norms)
    prb_copy.wait()
    left_copy.wait()

    def step(i, carry):
        done = []
        for k in range(PAIRS):
            target = targets[i * PAIRS + k]
            source = sources[i * PAIRS + k]
            which = lax.div(source, leaf_dev)
            span = pl.ds(pl.multiple_of(lax.rem(source, leaf_dev) * leaf_len, leaf_len), leaf_len)
            right = deep(pts[which, :, span], rows[which, :, span])
            source_prb = prb[which, :, span]
            left_at = jnp.minimum(target, leaf_dev - 1) * leaf_len
            for at in range(0, leaf_len, chunk):
                part = left[pl.ds(pl.multiple_of(left_at + at, chunk), chunk), :]
                block = jnp.exp(mm(part, right)).astype(BF16)
                done.append((target, at, mm_nt(source_prb, block)))
        for target, at, term in done:
            total[target, :, at : at + chunk] += term
        return carry

    lax.fori_loop(0, steps, step, 0)
    for leaf in range(leaf_dev):
        span = slice(leaf * leaf_len, (leaf + 1) * leaf_len)
        out[:, span] = total[leaf] + far[:, span]


def shape(dims, dtype):
    return jax.ShapeDtypeStruct(tuple(dims), dtype)


def per_device(points, probes, near_list, near_count, leaf_skel, local_skel, upper_skel):
    emb_width, shard_len = points.shape
    leaf_dev, slots = near_list.shape
    leaf_len = shard_len // leaf_dev
    skel = leaf_skel.shape[1]
    probe_num = probes.shape[0]
    levels = lax.axis_size("leaf").bit_length() - 1
    me = lax.axis_index("leaf").astype(jnp.int32).reshape(1)
    low_nodes = leaf_dev - 1
    all_nodes = 2 * leaf_dev - 1
    pts_rows = emb_width + 2 * PIECE
    vmem = pl.BlockSpec(memory_space=pltpu.VMEM)
    smem = pl.BlockSpec(memory_space=pltpu.SMEM)
    anywhere = pl.BlockSpec(memory_space=pl.ANY)
    left, near, far, halo_pts, halo_prb = pl.pallas_call(
        tree_body,
        out_shape=[
            shape((shard_len, DEEP), BF16),
            shape((leaf_dev, probe_num, leaf_len), F32),
            shape((probe_num, shard_len), F32),
            shape((3, emb_width, shard_len), BF16),
            shape((3, probe_num, shard_len), BF16),
        ],
        in_specs=[vmem] * 5,
        out_specs=[vmem] * 3 + [anywhere] * 2,
        scratch_shapes=[
            pltpu.VMEM((PIECE, shard_len), BF16),
            pltpu.VMEM((shard_len, skel), BF16),
            pltpu.VMEM((shard_len, skel), BF16),
            pltpu.VMEM((low_nodes, 2 * skel, skel), BF16),
            pltpu.VMEM((low_nodes, 2 * skel, skel), BF16),
            pltpu.VMEM((2 * low_nodes, probe_num, skel), F32),
            pltpu.VMEM((all_nodes, pts_rows, skel), BF16),
            pltpu.VMEM((all_nodes, probe_num, skel), BF16),
            pltpu.VMEM((levels, pts_rows + probe_num, skel), BF16),
            pltpu.VMEM((levels, pts_rows + probe_num, skel), BF16),
            pltpu.VMEM((levels, 2 * skel, skel), BF16),
            pltpu.VMEM((levels, 2 * skel, skel), BF16),
            pltpu.VMEM((levels, probe_num, skel), F32),
            pltpu.VMEM((all_nodes, probe_num, skel), F32),
            pltpu.SemaphoreType.DMA((2,)),
            pltpu.SemaphoreType.DMA((2 + 2 * leaf_dev,)),
            pltpu.SemaphoreType.DMA((2 + 2 * leaf_dev,)),
            pltpu.SemaphoreType.DMA((levels,)),
            pltpu.SemaphoreType.DMA((levels,)),
        ],
        compiler_params=pltpu.CompilerParams(
            vmem_limit_bytes=VMEM_LIMIT, collective_id=0, has_side_effects=True
        ),
        name="tree_and_halo",
    )(points, probes, leaf_skel, local_skel, upper_skel)

    pair_len = slots * leaf_dev + PAIRS
    return pl.pallas_call(
        near_body,
        out_shape=shape((probe_num, shard_len), F32),
        in_specs=[smem] * 3 + [anywhere] * 3 + [vmem] * 2,
        out_specs=vmem,
        scratch_shapes=[
            pltpu.VMEM((shard_len, DEEP), BF16),
            pltpu.VMEM((3, emb_width, shard_len), BF16),
            pltpu.VMEM((3, probe_num, shard_len), BF16),
            pltpu.VMEM((leaf_dev + 1, probe_num, leaf_len), F32),
            pltpu.VMEM((3, PIECE, shard_len), BF16),
            pltpu.SMEM((pair_len,), jnp.int32),
            pltpu.SMEM((pair_len,), jnp.int32),
            pltpu.SemaphoreType.DMA((5,)),
        ],
        compiler_params=pltpu.CompilerParams(vmem_limit_bytes=VMEM_LIMIT),
        name="near_field",
    )(me, near_list.T, near_count, left, halo_pts, halo_prb, near, far)


def solution(mesh):
    in_specs = (
        P(None, "leaf"),
        P(None, "leaf"),
        P("leaf", None),
        P("leaf"),
        P("leaf", None),
        P("leaf", None),
        P(),
    )
    return jax.shard_map(
        per_device, mesh=mesh, in_specs=in_specs, out_specs=P(None, "leaf"), check_vma=False
    )
```

```python
import jax
import jax.numpy as jnp
from jax import lax
from jax.experimental import pallas as pl
from jax.experimental.pallas import tpu as pltpu
from jax.sharding import PartitionSpec as P

F32 = jnp.float32
BF16 = jnp.bfloat16
DEEP = 256
PIECE = 16
PAIRS = 2
VMEM_LIMIT = 56 * 1024 * 1024
MESH = pl.DeviceIdType.MESH


def mm(left, right):
    return jnp.dot(left, right, preferred_element_type=F32)


def mm_nt(left, right):
    return lax.dot_general(left, right, (((1,), (1,)), ((), ())), preferred_element_type=F32)


def split(value):
    high = value.astype(BF16)
    low = (value - high.astype(F32)).astype(BF16)
    return high, low


def left_form(*blocks):
    return (deep(*blocks) * jnp.asarray(4.0 / blocks[0].shape[0], BF16)).T


def half_norms(pts):
    wide = pts.astype(F32)
    value = jnp.sum(wide * wide, axis=0, keepdims=True) * -0.5
    first = value.astype(BF16).astype(F32)
    rest = value - first
    second = rest.astype(BF16).astype(F32)
    third = (rest - second).astype(BF16).astype(F32)
    return first, second, third


def norm_rows(pieces, start):
    width = pieces[0].shape[1]
    row = lax.broadcasted_iota(jnp.int32, (PIECE, width), 0)
    rows = jnp.where(row < 6, 1.0, 0.0)
    for k, piece in enumerate(pieces):
        rows = jnp.where(row == start + k, piece, rows)
    return rows.astype(BF16)


def deep(*blocks):
    rows = sum(block.shape[0] for block in blocks)
    filler = jnp.zeros((DEEP - rows, blocks[0].shape[1]), BF16)
    return jnp.concatenate([*blocks, filler], axis=0)


def one_hot(pool, chosen):
    column = lax.broadcasted_iota(jnp.int32, (pool, chosen.shape[1]), 0)
    return jnp.where(column == chosen, 1.0, 0.0).astype(BF16)


def in_groups(total, size, step):
    size = min(size, total)
    if size == total:
        step(list(range(total)))
        return

    def body(i, carry):
        step([i * size + k for k in range(size)])
        return carry

    lax.fori_loop(0, total // size, body, 0)


def lockstep(chains):
    chains = list(chains)
    results = [None] * len(chains)
    running = list(range(len(chains)))
    while running:
        left_over = []
        for i in running:
            try:
                next(chains[i])
                left_over.append(i)
            except StopIteration as end:
                results[i] = end.value
        running = left_over
    return results


def block_term(part, right, source_prb):
    raw = mm(part, right)
    yield
    return mm_nt(source_prb, jnp.exp(raw).astype(BF16))


def tree_node(first, second, first_q, second_q, chosen, emb_width):
    skel = first.shape[1]
    right_end = emb_width + PIECE
    joined = jnp.concatenate([first, second], axis=1)
    parent = mm(joined, one_hot(2 * skel, chosen)).astype(BF16)
    left = left_form(joined[:emb_width], joined[right_end:])
    yield
    right = deep(jnp.concatenate([parent[:right_end], second[:right_end]], axis=1))
    raw = mm(left, right)
    yield
    up_high, up_low = split(jnp.exp(raw[:, :skel]))
    joined_q = jnp.concatenate([first_q, second_q], axis=1)
    yield
    parent_q = (mm(joined_q, up_high) + mm(joined_q, up_low)).astype(BF16)
    cross_high, cross_low = split(jnp.exp(raw[:skel, skel:]))
    couple_first = mm_nt(second_q, cross_high) + mm_nt(second_q, cross_low)
    couple_second = mm(first_q, cross_high) + mm(first_q, cross_low)
    return parent, parent_q, up_high, up_low, couple_first, couple_second


def spread_down(field, up_high, up_low):
    rows = field.shape[0]
    high, low = split(field)
    both = mm_nt(jnp.concatenate([high, low], axis=0), up_high)
    return both[:rows] + both[rows:] + mm_nt(high, up_low)


def tree_body(
    pts, prb, leaf_skel, local_skel, upper_skel,
    near, far, left_out, halo_pts, halo_prb,
    left, right_rows, lk_high, lk_low, up_high, up_low, couple, nodes, node_q,
    outbox, inbox, path_high, path_low, path_couple, fields,
    own_sem, halo_send, halo_recv, box_send, box_recv,
):
    emb_width = pts.shape[0]
    leaf_dev, skel = leaf_skel.shape
    leaf_len = pts.shape[1] // leaf_dev
    pts_rows = nodes.shape[1]
    levels = inbox.shape[0]
    dev_num = 1 << levels
    mine = lax.axis_index("leaf")
    bits = [lax.rem(lax.div(mine, 1 << level), 2) for level in range(levels)]
    partners = [mine + (1 - 2 * bits[level]) * (1 << level) for level in range(levels)]

    barrier = pltpu.get_barrier_semaphore()
    for peer in partners:
        pl.semaphore_signal(barrier, inc=1, device_id=(peer,), device_id_type=MESH)
    has_before = mine > 0
    has_after = mine < dev_num - 1
    crosses_before = jnp.logical_and(has_before, bits[0] == 0)
    crosses_after = jnp.logical_and(has_after, bits[0] == 1)

    @pl.when(crosses_before)
    def _():
        pl.semaphore_signal(barrier, inc=1, device_id=(mine - 1,), device_id_type=MESH)

    @pl.when(crosses_after)
    def _():
        pl.semaphore_signal(barrier, inc=1, device_id=(mine + 1,), device_id_type=MESH)

    pl.semaphore_wait(barrier, levels + jnp.where(jnp.logical_or(crosses_before, crosses_after), 1, 0))

    def halo_copy(which, source, target, peer):
        return pltpu.make_async_remote_copy(
            src_ref=source, dst_ref=target, send_sem=halo_send.at[which], recv_sem=halo_recv.at[which],
            device_id=(peer,), device_id_type=MESH,
        )

    def flow(first_sem, slot, peer):
        copies = [halo_copy(first_sem, prb, halo_prb.at[slot], peer)]
        for k in range(leaf_dev):
            span = pl.ds(k * leaf_len, leaf_len)
            copies.append(halo_copy(first_sem + 1 + k, pts.at[:, span], halo_pts.at[slot, :, span], peer))
        return copies

    to_after = flow(0, 0, mine + 1)
    to_before = flow(1 + leaf_dev, 2, mine - 1)
    late_after = jnp.logical_and(bits[0] == 1, bits[1] == 0)
    late_before = jnp.logical_and(bits[0] == 0, bits[1] == 1)

    def start_when(condition, copies):
        @pl.when(condition)
        def _():
            for copy in copies:
                copy.start()

    early_after = jnp.logical_and(has_after, jnp.logical_not(late_after))
    early_before = jnp.logical_and(has_before, jnp.logical_not(late_before))
    first_part = len(to_after) * 5 // 8

    def feed(level):
        if level == 0:
            start_when(early_after, to_after[first_part:])
            start_when(early_before, to_before[first_part:])
        count = len(to_after)
        part = slice((2 * level - 1) * count // (2 * levels - 1) if level else 0, (2 * level + 1) * count // (2 * levels - 1))
        start_when(late_after, to_after[part])
        start_when(late_before, to_before[part])

    start_when(early_after, to_after[:first_part])
    start_when(early_before, to_before[:first_part])
    own = [
        pltpu.make_async_copy(pts, halo_pts.at[1], own_sem.at[0]),
        pltpu.make_async_copy(prb, halo_prb.at[1], own_sem.at[1]),
    ]
    for copy in own:
        copy.start()

    def leaf_chain(i):
        span = pl.ds(pl.multiple_of(i * leaf_len, leaf_len), leaf_len)
        tile = pts[:, span]
        pieces = half_norms(tile)
        right = norm_rows(pieces, 3)
        left_rows = norm_rows(pieces, 0)
        tile_left = left_form(tile, left_rows)
        stacked = jnp.concatenate([tile, right, left_rows], axis=0)
        yield
        node = mm(stacked, one_hot(leaf_len, leaf_skel[pl.ds(i, 1), :])).astype(BF16)
        yield
        raw = mm(tile_left, deep(node[: emb_width + PIECE]))
        yield
        high, low = split(jnp.exp(raw))
        yield
        tile_prb = prb[:, span]
        charge = (mm(tile_prb, high) + mm(tile_prb, low)).astype(BF16)
        return span, right, tile_left, node, high, low, charge

    def leaf_step(ids):
        done = lockstep(leaf_chain(i) for i in ids)
        for i, (span, right, tile_left, node, high, low, charge) in zip(ids, done):
            left[span, :] = tile_left
            right_rows[:, span] = right
            lk_high[span, :] = high
            lk_low[span, :] = low
            nodes[i] = node
            node_q[i] = charge

    in_groups(leaf_dev, 4, leaf_step)
    left_copy = pltpu.make_async_copy(left, left_out, own_sem.at[2])
    left_copy.start()
    count = leaf_dev // 2
    row_base = 0
    while count:

        def level_step(ids, row_base=row_base):
            done = lockstep(
                tree_node(
                    nodes[2 * row], nodes[2 * row + 1], node_q[2 * row], node_q[2 * row + 1],
                    local_skel[pl.ds(row, 1), :], emb_width,
                )
                for row in [row_base + k for k in ids]
            )
            for k, (parent, parent_q, high, low, one, two) in zip(ids, done):
                row = row_base + k
                nodes[leaf_dev + row] = parent
                node_q[leaf_dev + row] = parent_q
                up_high[row] = high
                up_low[row] = low
                couple[2 * row] = one
                couple[2 * row + 1] = two

        in_groups(count, 4, level_step)
        row_base += count
        count //= 2
    top = 2 * leaf_dev - 2
    outbox[0, :pts_rows, :] = nodes[top]
    outbox[0, pts_rows:, :] = node_q[top]

    chunk = min(256, leaf_len)

    def own_pairs(i, carry):
        places = []
        chains = []
        for k in range(PAIRS):
            leaf = i * PAIRS + k
            start = pl.multiple_of(leaf * leaf_len, leaf_len)
            span = pl.ds(start, leaf_len)
            right = deep(pts[:, span], right_rows[:, span])
            for at in range(0, leaf_len, chunk):
                part = left[pl.ds(pl.multiple_of(start + at, chunk), chunk), :]
                places.append((leaf, at))
                chains.append(block_term(part, right, prb[:, span]))
        for (leaf, at), term in zip(places, lockstep(chains)):
            near[leaf, :, at : at + chunk] = term
        return carry

    groups = leaf_dev // PAIRS
    later = groups - groups // 4
    shares = [0] + [groups // 4 + level * later // (levels - 1) for level in range(levels)]
    for level in range(levels):
        exchange = pltpu.make_async_remote_copy(
            src_ref=outbox.at[level], dst_ref=inbox.at[level],
            send_sem=box_send.at[level], recv_sem=box_recv.at[level],
            device_id=(partners[level],), device_id_type=MESH,
        )
        exchange.start()
        feed(level)
        lax.fori_loop(shares[level], shares[level + 1], own_pairs, 0)
        exchange.wait()
        is_first = bits[level] == 0
        here = outbox[level]
        there = inbox[level]
        one = jnp.where(is_first, here, there)
        two = jnp.where(is_first, there, here)
        row = dev_num - (dev_num >> level) + lax.div(mine, 2 << level)
        [(parent, parent_q, high, low, couple_one, couple_two)] = lockstep(
            [
                tree_node(
                    one[:pts_rows], two[:pts_rows], one[pts_rows:], two[pts_rows:],
                    upper_skel[pl.ds(row, 1), :], emb_width,
                )
            ]
        )
        path_high[level] = high
        path_low[level] = low
        path_couple[level] = jnp.where(is_first, couple_one, couple_two)
        if level < levels - 1:
            outbox[level + 1, :pts_rows, :] = parent
            outbox[level + 1, pts_rows:, :] = parent_q

    field = jnp.zeros(path_couple.shape[1:], F32)
    for level in reversed(range(levels)):
        spread = spread_down(field, path_high[level], path_low[level])
        field = jnp.where(bits[level] == 0, spread[:, :skel], spread[:, skel:]) + path_couple[level]
    fields[top] = field
    count = 1
    row_base = leaf_dev - 2
    while count < leaf_dev:

        def down_step(ids, row_base=row_base):
            done = []
            for k in ids:
                row = row_base + k
                spread = spread_down(fields[leaf_dev + row], up_high[row], up_low[row])
                done.append((spread[:, :skel] + couple[2 * row], spread[:, skel:] + couple[2 * row + 1]))
            for k, (one, two) in zip(ids, done):
                fields[2 * (row_base + k)] = one
                fields[2 * (row_base + k) + 1] = two

        in_groups(count, 4, down_step)
        count *= 2
        row_base -= count

    def far_step(ids):
        for i in ids:
            span = pl.ds(pl.multiple_of(i * leaf_len, leaf_len), leaf_len)
            far[:, span] = spread_down(fields[i], lk_high[span, :], lk_low[span, :])

    in_groups(leaf_dev, 4, far_step)
    for copy in [*own, left_copy]:
        copy.wait()

    @pl.when(has_after)
    def _():
        for copy in to_after:
            copy.wait_send()
        for copy in to_before:
            copy.wait_recv()

    @pl.when(has_before)
    def _():
        for copy in to_before:
            copy.wait_send()
        for copy in to_after:
            copy.wait_recv()


def list_pairs(near_list, near_count, base, targets, sources):
    leaf_dev = near_list.shape[1]

    def of_leaf(leaf, found):
        def of_slot(slot, found):
            targets[found] = leaf
            sources[found] = jnp.clip(near_list[slot, leaf] - base, 0, 3 * leaf_dev - 1)
            return found + 1

        return lax.fori_loop(1, near_count[leaf], of_slot, found)

    found = lax.fori_loop(0, leaf_dev, of_leaf, 0)
    for k in range(PAIRS - 1):
        targets[found + k] = leaf_dev
        sources[found + k] = leaf_dev
    return (found + PAIRS - 1) // PAIRS


def near_body(
    me, near_list, near_count, left_in, pts_in, prb_in, own, far, out,
    left, pts, prb, total, rows, targets, sources, sems,
):
    leaf_dev = near_list.shape[1]
    leaf_len = total.shape[2]
    emb_width = pts.shape[1]
    chunk = min(256, leaf_len)
    pts_copies = [pltpu.make_async_copy(pts_in.at[k], pts.at[k], sems.at[k]) for k in range(3)]
    prb_copy = pltpu.make_async_copy(prb_in, prb, sems.at[3])
    left_copy = pltpu.make_async_copy(left_in, left, sems.at[4])
    for copy in [*pts_copies, prb_copy, left_copy]:
        copy.start()
    total[:leaf_dev] = own[...]
    total[leaf_dev] = jnp.zeros(total.shape[1:], F32)
    steps = list_pairs(near_list, near_count, (me[0] - 1) * leaf_dev, targets, sources)

    for which in range(3):
        pts_copies[which].wait()

        def norms(ids, which=which):
            for i in ids:
                span = pl.ds(pl.multiple_of(i * leaf_len, leaf_len), leaf_len)
                rows[which, :, span] = norm_rows(half_norms(pts[which, :, span]), 3)

        in_groups(leaf_dev, 4, norms)
    prb_copy.wait()
    left_copy.wait()

    def step(i, carry):
        places = []
        chains = []
        for k in range(PAIRS):
            target = targets[i * PAIRS + k]
            source = sources[i * PAIRS + k]
            which = lax.div(source, leaf_dev)
            span = pl.ds(pl.multiple_of(lax.rem(source, leaf_dev) * leaf_len, leaf_len), leaf_len)
            right = deep(pts[which, :, span], rows[which, :, span])
            source_prb = prb[which, :, span]
            left_at = jnp.minimum(target, leaf_dev - 1) * leaf_len
            for at in range(0, leaf_len, chunk):
                part = left[pl.ds(pl.multiple_of(left_at + at, chunk), chunk), :]
                places.append((target, at))
                chains.append(block_term(part, right, source_prb))
        for (target, at), term in zip(places, lockstep(chains)):
            total[target, :, at : at + chunk] += term
        return carry

    lax.fori_loop(0, steps, step, 0)
    for leaf in range(leaf_dev):
        span = slice(leaf * leaf_len, (leaf + 1) * leaf_len)
        out[:, span] = total[leaf] + far[:, span]


def shape(dims, dtype):
    return jax.ShapeDtypeStruct(tuple(dims), dtype)


def per_device(points, probes, near_list, near_count, leaf_skel, local_skel, upper_skel):
    emb_width, shard_len = points.shape
    leaf_dev, slots = near_list.shape
    leaf_len = shard_len // leaf_dev
    skel = leaf_skel.shape[1]
    probe_num = probes.shape[0]
    levels = lax.axis_size("leaf").bit_length() - 1
    me = lax.axis_index("leaf").astype(jnp.int32).reshape(1)
    low_nodes = leaf_dev - 1
    all_nodes = 2 * leaf_dev - 1
    pts_rows = emb_width + 2 * PIECE
    vmem = pl.BlockSpec(memory_space=pltpu.VMEM)
    smem = pl.BlockSpec(memory_space=pltpu.SMEM)
    anywhere = pl.BlockSpec(memory_space=pl.ANY)
    near, far, left, halo_pts, halo_prb = pl.pallas_call(
        tree_body,
        out_shape=[
            shape((leaf_dev, probe_num, leaf_len), F32),
            shape((probe_num, shard_len), F32),
            shape((shard_len, DEEP), BF16),
            shape((3, emb_width, shard_len), BF16),
            shape((3, probe_num, shard_len), BF16),
        ],
        in_specs=[vmem] * 5,
        out_specs=[vmem] * 2 + [anywhere] * 3,
        scratch_shapes=[
            pltpu.VMEM((shard_len, DEEP), BF16),
            pltpu.VMEM((PIECE, shard_len), BF16),
            pltpu.VMEM((shard_len, skel), BF16),
            pltpu.VMEM((shard_len, skel), BF16),
            pltpu.VMEM((low_nodes, 2 * skel, skel), BF16),
            pltpu.VMEM((low_nodes, 2 * skel, skel), BF16),
            pltpu.VMEM((2 * low_nodes, probe_num, skel), F32),
            pltpu.VMEM((all_nodes, pts_rows, skel), BF16),
            pltpu.VMEM((all_nodes, probe_num, skel), BF16),
            pltpu.VMEM((levels, pts_rows + probe_num, skel), BF16),
            pltpu.VMEM((levels, pts_rows + probe_num, skel), BF16),
            pltpu.VMEM((levels, 2 * skel, skel), BF16),
            pltpu.VMEM((levels, 2 * skel, skel), BF16),
            pltpu.VMEM((levels, probe_num, skel), F32),
            pltpu.VMEM((all_nodes, probe_num, skel), F32),
            pltpu.SemaphoreType.DMA((3,)),
            pltpu.SemaphoreType.DMA((2 + 2 * leaf_dev,)),
            pltpu.SemaphoreType.DMA((2 + 2 * leaf_dev,)),
            pltpu.SemaphoreType.DMA((levels,)),
            pltpu.SemaphoreType.DMA((levels,)),
        ],
        compiler_params=pltpu.CompilerParams(
            vmem_limit_bytes=VMEM_LIMIT, collective_id=0, has_side_effects=True
        ),
        name="tree_and_halo",
    )(points, probes, leaf_skel, local_skel, upper_skel)

    pair_len = slots * leaf_dev + PAIRS
    return pl.pallas_call(
        near_body,
        out_shape=shape((probe_num, shard_len), F32),
        in_specs=[smem] * 3 + [anywhere] * 3 + [vmem] * 2,
        out_specs=vmem,
        scratch_shapes=[
            pltpu.VMEM((shard_len, DEEP), BF16),
            pltpu.VMEM((3, emb_width, shard_len), BF16),
            pltpu.VMEM((3, probe_num, shard_len), BF16),
            pltpu.VMEM((leaf_dev + 1, probe_num, leaf_len), F32),
            pltpu.VMEM((3, PIECE, shard_len), BF16),
            pltpu.SMEM((pair_len,), jnp.int32),
            pltpu.SMEM((pair_len,), jnp.int32),
            pltpu.SemaphoreType.DMA((5,)),
        ],
        compiler_params=pltpu.CompilerParams(vmem_limit_bytes=VMEM_LIMIT),
        name="near_field",
    )(me, near_list.T, near_count, left, halo_pts, halo_prb, near, far)


def solution(mesh):
    in_specs = (
        P(None, "leaf"),
        P(None, "leaf"),
        P("leaf", None),
        P("leaf"),
        P("leaf", None),
        P("leaf", None),
        P(),
    )
    return jax.shard_map(
        per_device, mesh=mesh, in_specs=in_specs, out_specs=P(None, "leaf"), check_vma=False
    )
```

```python
import jax
import jax.numpy as jnp
from jax import lax
from jax.experimental import pallas as pl
from jax.experimental.pallas import tpu as pltpu
from jax.sharding import PartitionSpec as P

F32 = jnp.float32
BF16 = jnp.bfloat16
DEEP = 256
PIECE = 16
PAIRS = 2
NEAR_PAIRS = 4
VMEM_LIMIT = 56 * 1024 * 1024
MESH = pl.DeviceIdType.MESH


def mm(left, right):
    return jnp.dot(left, right, preferred_element_type=F32)


def mm_nt(left, right):
    return lax.dot_general(left, right, (((1,), (1,)), ((), ())), preferred_element_type=F32)


def split(value):
    high = value.astype(BF16)
    low = (value - high.astype(F32)).astype(BF16)
    return high, low


def left_form(*blocks):
    return (deep(*blocks) * jnp.asarray(4.0 / blocks[0].shape[0], BF16)).T


def half_norms(pts):
    wide = pts.astype(F32)
    value = jnp.sum(wide * wide, axis=0, keepdims=True) * -0.5
    first = value.astype(BF16).astype(F32)
    rest = value - first
    second = rest.astype(BF16).astype(F32)
    third = (rest - second).astype(BF16).astype(F32)
    return first, second, third


def norm_rows(pieces, start):
    width = pieces[0].shape[1]
    row = lax.broadcasted_iota(jnp.int32, (PIECE, width), 0)
    rows = jnp.where(row < 6, 1.0, 0.0)
    for k, piece in enumerate(pieces):
        rows = jnp.where(row == start + k, piece, rows)
    return rows.astype(BF16)


def deep(*blocks):
    rows = sum(block.shape[0] for block in blocks)
    filler = jnp.zeros((DEEP - rows, blocks[0].shape[1]), BF16)
    return jnp.concatenate([*blocks, filler], axis=0)


def one_hot(pool, chosen):
    column = lax.broadcasted_iota(jnp.int32, (pool, chosen.shape[1]), 0)
    return jnp.where(column == chosen, 1.0, 0.0).astype(BF16)


def in_groups(total, size, step):
    size = min(size, total)
    if size == total:
        step(list(range(total)))
        return

    def body(i, carry):
        step([i * size + k for k in range(size)])
        return carry

    lax.fori_loop(0, total // size, body, 0)


def lockstep(chains):
    chains = list(chains)
    results = [None] * len(chains)
    running = list(range(len(chains)))
    while running:
        left_over = []
        for i in running:
            try:
                next(chains[i])
                left_over.append(i)
            except StopIteration as end:
                results[i] = end.value
        running = left_over
    return results


def block_term(part, right, source_prb):
    raw = mm(part, right)
    yield
    return mm_nt(source_prb, jnp.exp(raw).astype(BF16))


def tree_node(first, second, first_q, second_q, chosen, emb_width):
    skel = first.shape[1]
    right_end = emb_width + PIECE
    joined = jnp.concatenate([first, second], axis=1)
    parent = mm(joined, one_hot(2 * skel, chosen)).astype(BF16)
    left = left_form(joined[:emb_width], joined[right_end:])
    yield
    right = deep(jnp.concatenate([parent[:right_end], second[:right_end]], axis=1))
    raw = mm(left, right)
    yield
    up_high, up_low = split(jnp.exp(raw[:, :skel]))
    joined_q = jnp.concatenate([first_q, second_q], axis=1)
    yield
    parent_q = (mm(joined_q, up_high) + mm(joined_q, up_low)).astype(BF16)
    cross_high, cross_low = split(jnp.exp(raw[:skel, skel:]))
    couple_first = mm_nt(second_q, cross_high) + mm_nt(second_q, cross_low)
    couple_second = mm(first_q, cross_high) + mm(first_q, cross_low)
    return parent, parent_q, up_high, up_low, couple_first, couple_second


def spread_down(field, up_high, up_low):
    rows = field.shape[0]
    high, low = split(field)
    both = mm_nt(jnp.concatenate([high, low], axis=0), up_high)
    return both[:rows] + both[rows:] + mm_nt(high, up_low)


def tree_body(
    pts, prb, leaf_skel, local_skel, upper_skel,
    near, far, left_out, halo_pts, halo_prb,
    left, right_rows, lk_high, lk_low, up_high, up_low, couple, nodes, node_q,
    outbox, inbox, path_high, path_low, path_couple, fields,
    own_sem, halo_send, halo_recv, box_send, box_recv,
):
    emb_width = pts.shape[0]
    leaf_dev, skel = leaf_skel.shape
    leaf_len = pts.shape[1] // leaf_dev
    pts_rows = nodes.shape[1]
    levels = inbox.shape[0]
    dev_num = 1 << levels
    mine = lax.axis_index("leaf")
    bits = [lax.rem(lax.div(mine, 1 << level), 2) for level in range(levels)]
    partners = [mine + (1 - 2 * bits[level]) * (1 << level) for level in range(levels)]

    barrier = pltpu.get_barrier_semaphore()
    for peer in partners:
        pl.semaphore_signal(barrier, inc=1, device_id=(peer,), device_id_type=MESH)
    has_before = mine > 0
    has_after = mine < dev_num - 1
    crosses_before = jnp.logical_and(has_before, bits[0] == 0)
    crosses_after = jnp.logical_and(has_after, bits[0] == 1)

    @pl.when(crosses_before)
    def _():
        pl.semaphore_signal(barrier, inc=1, device_id=(mine - 1,), device_id_type=MESH)

    @pl.when(crosses_after)
    def _():
        pl.semaphore_signal(barrier, inc=1, device_id=(mine + 1,), device_id_type=MESH)

    pl.semaphore_wait(barrier, levels + jnp.where(jnp.logical_or(crosses_before, crosses_after), 1, 0))

    def halo_copy(which, source, target, peer):
        return pltpu.make_async_remote_copy(
            src_ref=source, dst_ref=target, send_sem=halo_send.at[which], recv_sem=halo_recv.at[which],
            device_id=(peer,), device_id_type=MESH,
        )

    def flow(first_sem, slot, peer):
        copies = [halo_copy(first_sem, prb, halo_prb.at[slot], peer)]
        for k in range(leaf_dev):
            span = pl.ds(k * leaf_len, leaf_len)
            copies.append(halo_copy(first_sem + 1 + k, pts.at[:, span], halo_pts.at[slot, :, span], peer))
        return copies

    to_after = flow(0, 0, mine + 1)
    to_before = flow(1 + leaf_dev, 2, mine - 1)
    late_after = jnp.logical_and(bits[0] == 1, bits[1] == 0)
    late_before = jnp.logical_and(bits[0] == 0, bits[1] == 1)

    def start_when(condition, copies):
        @pl.when(condition)
        def _():
            for copy in copies:
                copy.start()

    early_after = jnp.logical_and(has_after, jnp.logical_not(late_after))
    early_before = jnp.logical_and(has_before, jnp.logical_not(late_before))
    step_len = -(-len(to_after) // levels)

    def feed(level):
        part = slice(level * step_len, (level + 1) * step_len)
        start_when(late_after, to_after[part])
        start_when(late_before, to_before[part])

    start_when(early_after, to_after)
    start_when(early_before, to_before)
    own = [
        pltpu.make_async_copy(pts, halo_pts.at[1], own_sem.at[0]),
        pltpu.make_async_copy(prb, halo_prb.at[1], own_sem.at[1]),
    ]
    for copy in own:
        copy.start()

    def leaf_chain(i):
        span = pl.ds(pl.multiple_of(i * leaf_len, leaf_len), leaf_len)
        tile = pts[:, span]
        pieces = half_norms(tile)
        right = norm_rows(pieces, 3)
        left_rows = norm_rows(pieces, 0)
        tile_left = left_form(tile, left_rows)
        stacked = jnp.concatenate([tile, right, left_rows], axis=0)
        yield
        node = mm(stacked, one_hot(leaf_len, leaf_skel[pl.ds(i, 1), :])).astype(BF16)
        yield
        raw = mm(tile_left, deep(node[: emb_width + PIECE]))
        yield
        high, low = split(jnp.exp(raw))
        yield
        tile_prb = prb[:, span]
        charge = (mm(tile_prb, high) + mm(tile_prb, low)).astype(BF16)
        return span, right, tile_left, node, high, low, charge

    def leaf_step(ids):
        done = lockstep(leaf_chain(i) for i in ids)
        for i, (span, right, tile_left, node, high, low, charge) in zip(ids, done):
            left[span, :] = tile_left
            right_rows[:, span] = right
            lk_high[span, :] = high
            lk_low[span, :] = low
            nodes[i] = node
            node_q[i] = charge

    in_groups(leaf_dev, 4, leaf_step)
    left_copy = pltpu.make_async_copy(left, left_out, own_sem.at[2])
    left_copy.start()
    count = leaf_dev // 2
    row_base = 0
    while count:

        def level_step(ids, row_base=row_base):
            done = lockstep(
                tree_node(
                    nodes[2 * row], nodes[2 * row + 1], node_q[2 * row], node_q[2 * row + 1],
                    local_skel[pl.ds(row, 1), :], emb_width,
                )
                for row in [row_base + k for k in ids]
            )
            for k, (parent, parent_q, high, low, one, two) in zip(ids, done):
                row = row_base + k
                nodes[leaf_dev + row] = parent
                node_q[leaf_dev + row] = parent_q
                up_high[row] = high
                up_low[row] = low
                couple[2 * row] = one
                couple[2 * row + 1] = two

        in_groups(count, 4, level_step)
        row_base += count
        count //= 2
    top = 2 * leaf_dev - 2
    outbox[0, :pts_rows, :] = nodes[top]
    outbox[0, pts_rows:, :] = node_q[top]

    chunk = min(256, leaf_len)

    def own_pairs(i, carry):
        places = []
        chains = []
        for k in range(PAIRS):
            leaf = i * PAIRS + k
            start = pl.multiple_of(leaf * leaf_len, leaf_len)
            span = pl.ds(start, leaf_len)
            right = deep(pts[:, span], right_rows[:, span])
            for at in range(0, leaf_len, chunk):
                part = left[pl.ds(pl.multiple_of(start + at, chunk), chunk), :]
                places.append((leaf, at))
                chains.append(block_term(part, right, prb[:, span]))
        for (leaf, at), term in zip(places, lockstep(chains)):
            near[leaf, :, at : at + chunk] = term
        return carry

    groups = leaf_dev // PAIRS
    later = groups - groups // 2
    shares = [0] + [groups // 2 + level * later // (levels - 1) for level in range(levels)]
    for level in range(levels):
        exchange = pltpu.make_async_remote_copy(
            src_ref=outbox.at[level], dst_ref=inbox.at[level],
            send_sem=box_send.at[level], recv_sem=box_recv.at[level],
            device_id=(partners[level],), device_id_type=MESH,
        )
        exchange.start()
        feed(level)
        lax.fori_loop(shares[level], shares[level + 1], own_pairs, 0)
        exchange.wait()
        is_first = bits[level] == 0
        here = outbox[level]
        there = inbox[level]
        one = jnp.where(is_first, here, there)
        two = jnp.where(is_first, there, here)
        row = dev_num - (dev_num >> level) + lax.div(mine, 2 << level)
        [(parent, parent_q, high, low, couple_one, couple_two)] = lockstep(
            [
                tree_node(
                    one[:pts_rows], two[:pts_rows], one[pts_rows:], two[pts_rows:],
                    upper_skel[pl.ds(row, 1), :], emb_width,
                )
            ]
        )
        path_high[level] = high
        path_low[level] = low
        path_couple[level] = jnp.where(is_first, couple_one, couple_two)
        if level < levels - 1:
            outbox[level + 1, :pts_rows, :] = parent
            outbox[level + 1, pts_rows:, :] = parent_q

    field = jnp.zeros(path_couple.shape[1:], F32)
    for level in reversed(range(levels)):
        spread = spread_down(field, path_high[level], path_low[level])
        field = jnp.where(bits[level] == 0, spread[:, :skel], spread[:, skel:]) + path_couple[level]
    fields[top] = field
    count = 1
    row_base = leaf_dev - 2
    while count < leaf_dev:

        def down_step(ids, row_base=row_base):
            done = []
            for k in ids:
                row = row_base + k
                spread = spread_down(fields[leaf_dev + row], up_high[row], up_low[row])
                done.append((spread[:, :skel] + couple[2 * row], spread[:, skel:] + couple[2 * row + 1]))
            for k, (one, two) in zip(ids, done):
                fields[2 * (row_base + k)] = one
                fields[2 * (row_base + k) + 1] = two

        in_groups(count, 4, down_step)
        count *= 2
        row_base -= count

    def far_step(ids):
        for i in ids:
            span = pl.ds(pl.multiple_of(i * leaf_len, leaf_len), leaf_len)
            far[:, span] = spread_down(fields[i], lk_high[span, :], lk_low[span, :])

    in_groups(leaf_dev, 4, far_step)
    for copy in [*own, left_copy]:
        copy.wait()

    @pl.when(has_after)
    def _():
        for copy in to_after:
            copy.wait_send()
        for copy in to_before:
            copy.wait_recv()

    @pl.when(has_before)
    def _():
        for copy in to_before:
            copy.wait_send()
        for copy in to_after:
            copy.wait_recv()


def list_pairs(near_list, near_count, base, targets, sources):
    leaf_dev = near_list.shape[1]

    def of_leaf(leaf, found):
        def of_slot(slot, found):
            targets[found] = leaf
            sources[found] = jnp.clip(near_list[slot, leaf] - base, 0, 3 * leaf_dev - 1)
            return found + 1

        return lax.fori_loop(1, near_count[leaf], of_slot, found)

    found = lax.fori_loop(0, leaf_dev, of_leaf, 0)
    for k in range(NEAR_PAIRS - 1):
        targets[found + k] = leaf_dev
        sources[found + k] = leaf_dev
    return (found + NEAR_PAIRS - 1) // NEAR_PAIRS


def near_body(
    me, near_list, near_count, left_in, pts_in, prb_in, own, far, out,
    left, pts, prb, total, rows, targets, sources, sems,
):
    leaf_dev = near_list.shape[1]
    leaf_len = total.shape[2]
    emb_width = pts.shape[1]
    chunk = min(256, leaf_len)
    pts_copies = [pltpu.make_async_copy(pts_in.at[k], pts.at[k], sems.at[k]) for k in range(3)]
    prb_copy = pltpu.make_async_copy(prb_in, prb, sems.at[3])
    left_copy = pltpu.make_async_copy(left_in, left, sems.at[4])
    for copy in [*pts_copies, prb_copy, left_copy]:
        copy.start()
    total[:leaf_dev] = own[...]
    total[leaf_dev] = jnp.zeros(total.shape[1:], F32)
    steps = list_pairs(near_list, near_count, (me[0] - 1) * leaf_dev, targets, sources)

    for which in range(3):
        pts_copies[which].wait()

        def norms(ids, which=which):
            for i in ids:
                span = pl.ds(pl.multiple_of(i * leaf_len, leaf_len), leaf_len)
                rows[which, :, span] = norm_rows(half_norms(pts[which, :, span]), 3)

        in_groups(leaf_dev, 4, norms)
    prb_copy.wait()
    left_copy.wait()

    def step(i, carry):
        places = []
        chains = []
        for k in range(NEAR_PAIRS):
            target = targets[i * NEAR_PAIRS + k]
            source = sources[i * NEAR_PAIRS + k]
            which = lax.div(source, leaf_dev)
            span = pl.ds(pl.multiple_of(lax.rem(source, leaf_dev) * leaf_len, leaf_len), leaf_len)
            right = deep(pts[which, :, span], rows[which, :, span])
            source_prb = prb[which, :, span]
            left_at = jnp.minimum(target, leaf_dev - 1) * leaf_len
            for at in range(0, leaf_len, chunk):
                part = left[pl.ds(pl.multiple_of(left_at + at, chunk), chunk), :]
                places.append((target, at))
                chains.append(block_term(part, right, source_prb))
        for (target, at), term in zip(places, lockstep(chains)):
            total[target, :, at : at + chunk] += term
        return carry

    lax.fori_loop(0, steps, step, 0)
    for leaf in range(leaf_dev):
        span = slice(leaf * leaf_len, (leaf + 1) * leaf_len)
        out[:, span] = total[leaf] + far[:, span]


def shape(dims, dtype):
    return jax.ShapeDtypeStruct(tuple(dims), dtype)


def per_device(points, probes, near_list, near_count, leaf_skel, local_skel, upper_skel):
    emb_width, shard_len = points.shape
    leaf_dev, slots = near_list.shape
    leaf_len = shard_len // leaf_dev
    skel = leaf_skel.shape[1]
    probe_num = probes.shape[0]
    levels = lax.axis_size("leaf").bit_length() - 1
    me = lax.axis_index("leaf").astype(jnp.int32).reshape(1)
    low_nodes = leaf_dev - 1
    all_nodes = 2 * leaf_dev - 1
    pts_rows = emb_width + 2 * PIECE
    vmem = pl.BlockSpec(memory_space=pltpu.VMEM)
    smem = pl.BlockSpec(memory_space=pltpu.SMEM)
    anywhere = pl.BlockSpec(memory_space=pl.ANY)
    near, far, left, halo_pts, halo_prb = pl.pallas_call(
        tree_body,
        out_shape=[
            shape((leaf_dev, probe_num, leaf_len), F32),
            shape((probe_num, shard_len), F32),
            shape((shard_len, DEEP), BF16),
            shape((3, emb_width, shard_len), BF16),
            shape((3, probe_num, shard_len), BF16),
        ],
        in_specs=[vmem] * 5,
        out_specs=[vmem] * 2 + [anywhere] * 3,
        scratch_shapes=[
            pltpu.VMEM((shard_len, DEEP), BF16),
            pltpu.VMEM((PIECE, shard_len), BF16),
            pltpu.VMEM((shard_len, skel), BF16),
            pltpu.VMEM((shard_len, skel), BF16),
            pltpu.VMEM((low_nodes, 2 * skel, skel), BF16),
            pltpu.VMEM((low_nodes, 2 * skel, skel), BF16),
            pltpu.VMEM((2 * low_nodes, probe_num, skel), F32),
            pltpu.VMEM((all_nodes, pts_rows, skel), BF16),
            pltpu.VMEM((all_nodes, probe_num, skel), BF16),
            pltpu.VMEM((levels, pts_rows + probe_num, skel), BF16),
            pltpu.VMEM((levels, pts_rows + probe_num, skel), BF16),
            pltpu.VMEM((levels, 2 * skel, skel), BF16),
            pltpu.VMEM((levels, 2 * skel, skel), BF16),
            pltpu.VMEM((levels, probe_num, skel), F32),
            pltpu.VMEM((all_nodes, probe_num, skel), F32),
            pltpu.SemaphoreType.DMA((3,)),
            pltpu.SemaphoreType.DMA((2 + 2 * leaf_dev,)),
            pltpu.SemaphoreType.DMA((2 + 2 * leaf_dev,)),
            pltpu.SemaphoreType.DMA((levels,)),
            pltpu.SemaphoreType.DMA((levels,)),
        ],
        compiler_params=pltpu.CompilerParams(
            vmem_limit_bytes=VMEM_LIMIT, collective_id=0, has_side_effects=True
        ),
        name="tree_and_halo",
    )(points, probes, leaf_skel, local_skel, upper_skel)

    pair_len = slots * leaf_dev + NEAR_PAIRS
    return pl.pallas_call(
        near_body,
        out_shape=shape((probe_num, shard_len), F32),
        in_specs=[smem] * 3 + [anywhere] * 3 + [vmem] * 2,
        out_specs=vmem,
        scratch_shapes=[
            pltpu.VMEM((shard_len, DEEP), BF16),
            pltpu.VMEM((3, emb_width, shard_len), BF16),
            pltpu.VMEM((3, probe_num, shard_len), BF16),
            pltpu.VMEM((leaf_dev + 1, probe_num, leaf_len), F32),
            pltpu.VMEM((3, PIECE, shard_len), BF16),
            pltpu.SMEM((pair_len,), jnp.int32),
            pltpu.SMEM((pair_len,), jnp.int32),
            pltpu.SemaphoreType.DMA((5,)),
        ],
        compiler_params=pltpu.CompilerParams(vmem_limit_bytes=VMEM_LIMIT),
        name="near_field",
    )(me, near_list.T, near_count, left, halo_pts, halo_prb, near, far)


def solution(mesh):
    in_specs = (
        P(None, "leaf"),
        P(None, "leaf"),
        P("leaf", None),
        P("leaf"),
        P("leaf", None),
        P("leaf", None),
        P(),
    )
    return jax.shard_map(
        per_device, mesh=mesh, in_specs=in_specs, out_specs=P(None, "leaf"), check_vma=False
    )
```

```python
import jax
import jax.numpy as jnp
from jax import lax
from jax.experimental import pallas as pl
from jax.experimental.pallas import tpu as pltpu
from jax.sharding import PartitionSpec as P

F32 = jnp.float32
BF16 = jnp.bfloat16
DEEP = 256
PIECE = 16
PAIRS = 2
NEAR_PAIRS = 4
VMEM_LIMIT = 56 * 1024 * 1024
MESH = pl.DeviceIdType.MESH


def mm(left, right):
    return jnp.dot(left, right, preferred_element_type=F32)


def mm_nt(left, right):
    return lax.dot_general(left, right, (((1,), (1,)), ((), ())), preferred_element_type=F32)


def split(value):
    high = value.astype(BF16)
    low = (value - high.astype(F32)).astype(BF16)
    return high, low


def left_form(*blocks):
    return (deep(*blocks) * jnp.asarray(4.0 / blocks[0].shape[0], BF16)).T


def half_norms(pts):
    wide = pts.astype(F32)
    value = jnp.sum(wide * wide, axis=0, keepdims=True) * -0.5
    first = value.astype(BF16).astype(F32)
    rest = value - first
    second = rest.astype(BF16).astype(F32)
    third = (rest - second).astype(BF16).astype(F32)
    return first, second, third


def norm_rows(pieces, start):
    width = pieces[0].shape[1]
    row = lax.broadcasted_iota(jnp.int32, (PIECE, width), 0)
    rows = jnp.where(row < 6, 1.0, 0.0)
    for k, piece in enumerate(pieces):
        rows = jnp.where(row == start + k, piece, rows)
    return rows.astype(BF16)


def deep(*blocks):
    rows = sum(block.shape[0] for block in blocks)
    filler = jnp.zeros((DEEP - rows, blocks[0].shape[1]), BF16)
    return jnp.concatenate([*blocks, filler], axis=0)


def one_hot(pool, chosen):
    column = lax.broadcasted_iota(jnp.int32, (pool, chosen.shape[1]), 0)
    return jnp.where(column == chosen, 1.0, 0.0).astype(BF16)


def in_groups(total, size, step):
    size = min(size, total)
    if size == total:
        step(list(range(total)))
        return

    def body(i, carry):
        step([i * size + k for k in range(size)])
        return carry

    lax.fori_loop(0, total // size, body, 0)


def lockstep(chains):
    chains = list(chains)
    results = [None] * len(chains)
    running = list(range(len(chains)))
    while running:
        left_over = []
        for i in running:
            try:
                next(chains[i])
                left_over.append(i)
            except StopIteration as end:
                results[i] = end.value
        running = left_over
    return results


def block_term(part, right, source_prb):
    raw = mm(part, right)
    yield
    return mm_nt(source_prb, jnp.exp(raw).astype(BF16))


def tree_node(first, second, first_q, second_q, chosen, emb_width):
    skel = first.shape[1]
    right_end = emb_width + PIECE
    joined = jnp.concatenate([first, second], axis=1)
    parent = mm(joined, one_hot(2 * skel, chosen)).astype(BF16)
    left = left_form(joined[:emb_width], joined[right_end:])
    right = deep(jnp.concatenate([parent[:right_end], second[:right_end]], axis=1))
    raw = mm(left, right)
    up_high, up_low = split(jnp.exp(raw[:, :skel]))
    joined_q = jnp.concatenate([first_q, second_q], axis=1)
    parent_q = (mm(joined_q, up_high) + mm(joined_q, up_low)).astype(BF16)
    cross_high, cross_low = split(jnp.exp(raw[:skel, skel:]))
    couple_first = mm_nt(second_q, cross_high) + mm_nt(second_q, cross_low)
    couple_second = mm(first_q, cross_high) + mm(first_q, cross_low)
    return parent, parent_q, up_high, up_low, couple_first, couple_second


def spread_down(field, up_high, up_low):
    rows = field.shape[0]
    high, low = split(field)
    both = mm_nt(jnp.concatenate([high, low], axis=0), up_high)
    return both[:rows] + both[rows:] + mm_nt(high, up_low)


def tree_body(
    pts, prb, leaf_skel, local_skel, upper_skel,
    left, near, far, halo_pts, halo_prb,
    right_rows, lk_high, lk_low, up_high, up_low, couple, nodes, node_q,
    outbox, inbox, path_high, path_low, path_couple, fields,
    own_sem, halo_send, halo_recv, box_send, box_recv,
):
    emb_width = pts.shape[0]
    leaf_dev, skel = leaf_skel.shape
    leaf_len = pts.shape[1] // leaf_dev
    pts_rows = nodes.shape[1]
    levels = inbox.shape[0]
    dev_num = 1 << levels
    mine = lax.axis_index("leaf")
    bits = [lax.rem(lax.div(mine, 1 << level), 2) for level in range(levels)]
    partners = [mine + (1 - 2 * bits[level]) * (1 << level) for level in range(levels)]

    barrier = pltpu.get_barrier_semaphore()
    for peer in partners:
        pl.semaphore_signal(barrier, inc=1, device_id=(peer,), device_id_type=MESH)
    has_before = mine > 0
    has_after = mine < dev_num - 1
    crosses_before = jnp.logical_and(has_before, bits[0] == 0)
    crosses_after = jnp.logical_and(has_after, bits[0] == 1)

    @pl.when(crosses_before)
    def _():
        pl.semaphore_signal(barrier, inc=1, device_id=(mine - 1,), device_id_type=MESH)

    @pl.when(crosses_after)
    def _():
        pl.semaphore_signal(barrier, inc=1, device_id=(mine + 1,), device_id_type=MESH)

    pl.semaphore_wait(barrier, levels + jnp.where(jnp.logical_or(crosses_before, crosses_after), 1, 0))

    def halo_copy(which, source, target, peer):
        return pltpu.make_async_remote_copy(
            src_ref=source, dst_ref=target, send_sem=halo_send.at[which], recv_sem=halo_recv.at[which],
            device_id=(peer,), device_id_type=MESH,
        )

    def flow(first_sem, slot, peer):
        copies = [halo_copy(first_sem, prb, halo_prb.at[slot], peer)]
        for k in range(leaf_dev):
            span = pl.ds(k * leaf_len, leaf_len)
            copies.append(halo_copy(first_sem + 1 + k, pts.at[:, span], halo_pts.at[slot, :, span], peer))
        return copies

    to_after = flow(0, 0, mine + 1)
    to_before = flow(1 + leaf_dev, 2, mine - 1)
    late_after = jnp.logical_and(bits[0] == 1, bits[1] == 0)
    late_before = jnp.logical_and(bits[0] == 0, bits[1] == 1)

    def start_when(condition, copies):
        @pl.when(condition)
        def _():
            for copy in copies:
                copy.start()

    def feed(level):
        part = slice(level * len(to_after) // levels, (level + 1) * len(to_after) // levels)
        start_when(late_after, to_after[part])
        start_when(late_before, to_before[part])

    start_when(jnp.logical_and(has_after, jnp.logical_not(late_after)), to_after)
    start_when(jnp.logical_and(has_before, jnp.logical_not(late_before)), to_before)
    own = [
        pltpu.make_async_copy(pts, halo_pts.at[1], own_sem.at[0]),
        pltpu.make_async_copy(prb, halo_prb.at[1], own_sem.at[1]),
    ]
    for copy in own:
        copy.start()

    def leaf_step(ids):
        done = []
        for i in ids:
            span = pl.ds(pl.multiple_of(i * leaf_len, leaf_len), leaf_len)
            tile = pts[:, span]
            pieces = half_norms(tile)
            right = norm_rows(pieces, 3)
            left_rows = norm_rows(pieces, 0)
            tile_left = left_form(tile, left_rows)
            stacked = jnp.concatenate([tile, right, left_rows], axis=0)
            node = mm(stacked, one_hot(leaf_len, leaf_skel[pl.ds(i, 1), :])).astype(BF16)
            raw = mm(tile_left, deep(node[: emb_width + PIECE]))
            high, low = split(jnp.exp(raw))
            tile_prb = prb[:, span]
            charge = (mm(tile_prb, high) + mm(tile_prb, low)).astype(BF16)
            done.append((span, right, tile_left, node, high, low, charge))
        for i, (span, right, tile_left, node, high, low, charge) in zip(ids, done):
            left[span, :] = tile_left
            right_rows[:, span] = right
            lk_high[span, :] = high
            lk_low[span, :] = low
            nodes[i] = node
            node_q[i] = charge

    in_groups(leaf_dev, 4, leaf_step)
    count = leaf_dev // 2
    row_base = 0
    while count:

        def level_step(ids, row_base=row_base):
            done = []
            for k in ids:
                row = row_base + k
                done.append(
                    tree_node(
                        nodes[2 * row], nodes[2 * row + 1], node_q[2 * row], node_q[2 * row + 1],
                        local_skel[pl.ds(row, 1), :], emb_width,
                    )
                )
            for k, (parent, parent_q, high, low, one, two) in zip(ids, done):
                row = row_base + k
                nodes[leaf_dev + row] = parent
                node_q[leaf_dev + row] = parent_q
                up_high[row] = high
                up_low[row] = low
                couple[2 * row] = one
                couple[2 * row + 1] = two

        in_groups(count, 4, level_step)
        row_base += count
        count //= 2
    top = 2 * leaf_dev - 2
    outbox[0, :pts_rows, :] = nodes[top]
    outbox[0, pts_rows:, :] = node_q[top]

    chunk = min(256, leaf_len)

    def own_pairs(i, carry):
        terms = []
        for k in range(PAIRS):
            leaf = i * PAIRS + k
            start = pl.multiple_of(leaf * leaf_len, leaf_len)
            span = pl.ds(start, leaf_len)
            right = deep(pts[:, span], right_rows[:, span])
            for at in range(0, leaf_len, chunk):
                part = left[pl.ds(pl.multiple_of(start + at, chunk), chunk), :]
                block = jnp.exp(mm(part, right)).astype(BF16)
                terms.append((leaf, at, mm_nt(prb[:, span], block)))
        for leaf, at, term in terms:
            near[leaf, :, at : at + chunk] = term
        return carry

    groups = leaf_dev // PAIRS
    later = groups - groups // 2
    shares = [0] + [groups // 2 + level * later // (levels - 1) for level in range(levels)]
    for level in range(levels):
        exchange = pltpu.make_async_remote_copy(
            src_ref=outbox.at[level], dst_ref=inbox.at[level],
            send_sem=box_send.at[level], recv_sem=box_recv.at[level],
            device_id=(partners[level],), device_id_type=MESH,
        )
        exchange.start()
        feed(level)
        lax.fori_loop(shares[level], shares[level + 1], own_pairs, 0)
        exchange.wait()
        is_first = bits[level] == 0
        here = outbox[level]
        there = inbox[level]
        one = jnp.where(is_first, here, there)
        two = jnp.where(is_first, there, here)
        row = dev_num - (dev_num >> level) + lax.div(mine, 2 << level)
        parent, parent_q, high, low, couple_one, couple_two = tree_node(
            one[:pts_rows], two[:pts_rows], one[pts_rows:], two[pts_rows:],
            upper_skel[pl.ds(row, 1), :], emb_width,
        )
        path_high[level] = high
        path_low[level] = low
        path_couple[level] = jnp.where(is_first, couple_one, couple_two)
        if level < levels - 1:
            outbox[level + 1, :pts_rows, :] = parent
            outbox[level + 1, pts_rows:, :] = parent_q

    field = jnp.zeros(path_couple.shape[1:], F32)
    for level in reversed(range(levels)):
        spread = spread_down(field, path_high[level], path_low[level])
        field = jnp.where(bits[level] == 0, spread[:, :skel], spread[:, skel:]) + path_couple[level]
    fields[top] = field
    count = 1
    row_base = leaf_dev - 2
    while count < leaf_dev:

        def down_step(ids, row_base=row_base):
            done = []
            for k in ids:
                row = row_base + k
                spread = spread_down(fields[leaf_dev + row], up_high[row], up_low[row])
                done.append((spread[:, :skel] + couple[2 * row], spread[:, skel:] + couple[2 * row + 1]))
            for k, (one, two) in zip(ids, done):
                fields[2 * (row_base + k)] = one
                fields[2 * (row_base + k) + 1] = two

        in_groups(count, 4, down_step)
        count *= 2
        row_base -= count

    def far_step(ids):
        for i in ids:
            span = pl.ds(pl.multiple_of(i * leaf_len, leaf_len), leaf_len)
            far[:, span] = spread_down(fields[i], lk_high[span, :], lk_low[span, :])

    in_groups(leaf_dev, 4, far_step)
    for copy in own:
        copy.wait()

    @pl.when(has_after)
    def _():
        for copy in to_after:
            copy.wait_send()
        for copy in to_before:
            copy.wait_recv()

    @pl.when(has_before)
    def _():
        for copy in to_before:
            copy.wait_send()
        for copy in to_after:
            copy.wait_recv()


def list_pairs(near_list, near_count, base, targets, sources):
    leaf_dev = near_list.shape[1]

    def of_leaf(leaf, found):
        def of_slot(slot, found):
            targets[found] = leaf
            sources[found] = jnp.clip(near_list[slot, leaf] - base, 0, 3 * leaf_dev - 1)
            return found + 1

        return lax.fori_loop(1, near_count[leaf], of_slot, found)

    found = lax.fori_loop(0, leaf_dev, of_leaf, 0)
    for k in range(NEAR_PAIRS - 1):
        targets[found + k] = leaf_dev
        sources[found + k] = leaf_dev
    return (found + NEAR_PAIRS - 1) // NEAR_PAIRS


def near_body(
    me, near_list, near_count, left_in, pts_in, prb_in, own, far, out,
    left, pts, prb, total, rows, targets, sources, sems,
):
    leaf_dev = near_list.shape[1]
    leaf_len = total.shape[2]
    emb_width = pts.shape[1]
    chunk = min(256, leaf_len)
    pts_copies = [pltpu.make_async_copy(pts_in.at[k], pts.at[k], sems.at[k]) for k in range(3)]
    prb_copy = pltpu.make_async_copy(prb_in, prb, sems.at[3])
    left_copy = pltpu.make_async_copy(left_in, left, sems.at[4])
    for copy in [*pts_copies, prb_copy, left_copy]:
        copy.start()
    total[:leaf_dev] = own[...]
    total[leaf_dev] = jnp.zeros(total.shape[1:], F32)
    steps = list_pairs(near_list, near_count, (me[0] - 1) * leaf_dev, targets, sources)

    for which in range(3):
        pts_copies[which].wait()

        def norms(ids, which=which):
            for i in ids:
                span = pl.ds(pl.multiple_of(i * leaf_len, leaf_len), leaf_len)
                rows[which, :, span] = norm_rows(half_norms(pts[which, :, span]), 3)

        in_groups(leaf_dev, 4, norms)
    prb_copy.wait()
    left_copy.wait()

    def step(i, carry):
        places = []
        chains = []
        for k in range(NEAR_PAIRS):
            target = targets[i * NEAR_PAIRS + k]
            source = sources[i * NEAR_PAIRS + k]
            which = lax.div(source, leaf_dev)
            span = pl.ds(pl.multiple_of(lax.rem(source, leaf_dev) * leaf_len, leaf_len), leaf_len)
            right = deep(pts[which, :, span], rows[which, :, span])
            source_prb = prb[which, :, span]
            left_at = jnp.minimum(target, leaf_dev - 1) * leaf_len
            for at in range(0, leaf_len, chunk):
                part = left[pl.ds(pl.multiple_of(left_at + at, chunk), chunk), :]
                places.append((target, at))
                chains.append(block_term(part, right, source_prb))
        for (target, at), term in zip(places, lockstep(chains)):
            total[target, :, at : at + chunk] += term
        return carry

    lax.fori_loop(0, steps, step, 0)
    for leaf in range(leaf_dev):
        span = slice(leaf * leaf_len, (leaf + 1) * leaf_len)
        out[:, span] = total[leaf] + far[:, span]


def shape(dims, dtype):
    return jax.ShapeDtypeStruct(tuple(dims), dtype)


def per_device(points, probes, near_list, near_count, leaf_skel, local_skel, upper_skel):
    emb_width, shard_len = points.shape
    leaf_dev, slots = near_list.shape
    leaf_len = shard_len // leaf_dev
    skel = leaf_skel.shape[1]
    probe_num = probes.shape[0]
    levels = lax.axis_size("leaf").bit_length() - 1
    me = lax.axis_index("leaf").astype(jnp.int32).reshape(1)
    low_nodes = leaf_dev - 1
    all_nodes = 2 * leaf_dev - 1
    pts_rows = emb_width + 2 * PIECE
    vmem = pl.BlockSpec(memory_space=pltpu.VMEM)
    smem = pl.BlockSpec(memory_space=pltpu.SMEM)
    anywhere = pl.BlockSpec(memory_space=pl.ANY)
    left, near, far, halo_pts, halo_prb = pl.pallas_call(
        tree_body,
        out_shape=[
            shape((shard_len, DEEP), BF16),
            shape((leaf_dev, probe_num, leaf_len), F32),
            shape((probe_num, shard_len), F32),
            shape((3, emb_width, shard_len), BF16),
            shape((3, probe_num, shard_len), BF16),
        ],
        in_specs=[vmem] * 5,
        out_specs=[vmem] * 3 + [anywhere] * 2,
        scratch_shapes=[
            pltpu.VMEM((PIECE, shard_len), BF16),
            pltpu.VMEM((shard_len, skel), BF16),
            pltpu.VMEM((shard_len, skel), BF16),
            pltpu.VMEM((low_nodes, 2 * skel, skel), BF16),
            pltpu.VMEM((low_nodes, 2 * skel, skel), BF16),
            pltpu.VMEM((2 * low_nodes, probe_num, skel), F32),
            pltpu.VMEM((all_nodes, pts_rows, skel), BF16),
            pltpu.VMEM((all_nodes, probe_num, skel), BF16),
            pltpu.VMEM((levels, pts_rows + probe_num, skel), BF16),
            pltpu.VMEM((levels, pts_rows + probe_num, skel), BF16),
            pltpu.VMEM((levels, 2 * skel, skel), BF16),
            pltpu.VMEM((levels, 2 * skel, skel), BF16),
            pltpu.VMEM((levels, probe_num, skel), F32),
            pltpu.VMEM((all_nodes, probe_num, skel), F32),
            pltpu.SemaphoreType.DMA((2,)),
            pltpu.SemaphoreType.DMA((2 + 2 * leaf_dev,)),
            pltpu.SemaphoreType.DMA((2 + 2 * leaf_dev,)),
            pltpu.SemaphoreType.DMA((levels,)),
            pltpu.SemaphoreType.DMA((levels,)),
        ],
        compiler_params=pltpu.CompilerParams(
            vmem_limit_bytes=VMEM_LIMIT, collective_id=0, has_side_effects=True
        ),
        name="tree_and_halo",
    )(points, probes, leaf_skel, local_skel, upper_skel)

    pair_len = slots * leaf_dev + NEAR_PAIRS
    return pl.pallas_call(
        near_body,
        out_shape=shape((probe_num, shard_len), F32),
        in_specs=[smem] * 3 + [anywhere] * 3 + [vmem] * 2,
        out_specs=vmem,
        scratch_shapes=[
            pltpu.VMEM((shard_len, DEEP), BF16),
            pltpu.VMEM((3, emb_width, shard_len), BF16),
            pltpu.VMEM((3, probe_num, shard_len), BF16),
            pltpu.VMEM((leaf_dev + 1, probe_num, leaf_len), F32),
            pltpu.VMEM((3, PIECE, shard_len), BF16),
            pltpu.SMEM((pair_len,), jnp.int32),
            pltpu.SMEM((pair_len,), jnp.int32),
            pltpu.SemaphoreType.DMA((5,)),
        ],
        compiler_params=pltpu.CompilerParams(vmem_limit_bytes=VMEM_LIMIT),
        name="near_field",
    )(me, near_list.T, near_count, left, halo_pts, halo_prb, near, far)


def solution(mesh):
    in_specs = (
        P(None, "leaf"),
        P(None, "leaf"),
        P("leaf", None),
        P("leaf"),
        P("leaf", None),
        P("leaf", None),
        P(),
    )
    return jax.shard_map(
        per_device, mesh=mesh, in_specs=in_specs, out_specs=P(None, "leaf"), check_vma=False
    )
```
